128 devices in a mesh: prow: 8 (over z, core), pcol: 16 (over x, y).
Axes of the slice: x: 4, y: 4, z: 4, core: 2. Of those that a mesh axis runs over, the one named last changes fastest.
Arguments:
- ancestor_inverse: float32 [16384, 8, 16, 128], P('prow', None, 'pcol'), as said below
- lower_panel: float32 [16384, 2048], P(('prow', 'pcol')), as said below
- structure: int32 [16, 64], replicated, may hold values from 0 to 127, as said below
- pivot_inverse: float32 [16, 128, 128], replicated, may hold values from -6 to 6
Outputs:
- panel_inverse: float32 [16384, 2048], P(('prow', 'pcol'))
- diag_inverse: float32 [16, 128, 128], replicated
The draws below stay inside these ranges and needn't reach their ends.
Inputs may be any that keep to these rules, and one draw needn't show every extreme that they name: `structure`: each row lists 64 distinct ancestor tiles in increasing order; tiles 0 and 127 are in every row. ancestor_inverse, read as an 16384 x 16384 matrix, is symmetric. `lower_panel`: tile row j of column block b is zero unless tile j is listed in row b of structure.
All inputs are finite; a program needn't handle non-finite values.
Results may differ from the reference program's by a relative error of at most 0.000071.
Values sent between devices are 32-bit elements; how exact they have to be, the bound alone decides.
A program may use at most 128 MiB of HBM per device.

```python
import math
import jax
import jax.numpy as jnp
from jax import lax

W = 128
NA = 128
S = 64
B = 16
UNIT = 128
N_PROW = 8
N_PCOL = 16


def structure_of(key):
    noise = jax.random.randint(key, (B, NA), 0, NA)
    tiles = jnp.arange(NA, dtype=jnp.int32)
    score = (noise + tiles[None, :]) * NA + tiles[None, :]
    score = jnp.where(tiles[None, :] == NA - 1, 4 * NA * NA, score)
    score = jnp.where(tiles[None, :] == 0, 4 * NA * NA - 1, score)
    chosen = lax.top_k(score, S)[1]
    return jnp.sort(chosen, axis=1).astype(jnp.int32)


def draw_structure(key, part):
    return structure_of(key)


def draw_lower_panel(key, part):
    listed = structure_of(key)
    key = jax.random.fold_in(key, 2)
    order = NA * W
    tiles = jnp.arange(NA, dtype=jnp.int32)
    member = jnp.any(listed[None, :, :] == tiles[:, None, None], axis=2).astype(jnp.float32)
    row_member = jnp.repeat(member, W, axis=0)
    values = jax.random.normal(key, (order, B * W), jnp.float32)
    shaped = values.reshape(order, B, W) * row_member[:, :, None] * 0.02
    return shaped.reshape(order, B * W)


def draw_ancestor_inverse(key, part):
    key = jax.random.fold_in(key, 3)
    order = NA * W
    base = jax.random.normal(key, (order, order), jnp.float32)
    rows = jnp.arange(order, dtype=jnp.int32)
    both = (base + base.T) * (0.8 / math.sqrt(2.0 * order))
    both = both + jnp.where(rows[:, None] == rows[None, :], 2.0, 0.0)
    return both.reshape(order, N_PROW, N_PCOL, UNIT)


def gaussian(own_key, extent, scale, reach, kind=jnp.bfloat16):
    entries = jax.random.normal(own_key, extent, jnp.float32) * scale
    return jnp.minimum(jnp.maximum(entries, -reach), reach).astype(kind)


def setup_inputs(seed: int = 0) -> dict:
    arg_keys = jax.random.split(jax.random.key(seed), 5)
    return {
        "ancestor_inverse": draw_ancestor_inverse(jax.random.fold_in(arg_keys[4], 71), 0),
        "lower_panel": draw_lower_panel(jax.random.fold_in(arg_keys[4], 71), 0),
        "structure": draw_structure(jax.random.fold_in(arg_keys[4], 71), 0),
        "pivot_inverse": gaussian(arg_keys[3], (B, W, W), 1.0, 6.0, jnp.float32),
    }


def reference(ancestor_inverse, lower_panel, structure, pivot_inverse):
    order = NA * W
    ainv = ancestor_inverse.reshape(order, order)
    product = jnp.dot(ainv, lower_panel, precision=lax.Precision.HIGHEST, preferred_element_type=jnp.float32)
    tiles = jnp.arange(NA, dtype=jnp.int32)
    member = jnp.any(structure[None, :, :] == tiles[:, None, None], axis=2).astype(jnp.float32)
    row_member = jnp.repeat(member, W, axis=0)
    panel = -(product.reshape(order, B, W) * row_member[:, :, None])
    lower = lower_panel.reshape(order, B, W)
    correction = jnp.einsum("rbi,rbj->bij", lower, panel, precision=lax.Precision.HIGHEST, preferred_element_type=jnp.float32)
    diag_inverse = pivot_inverse - correction
    return panel.reshape(order, B * W), diag_inverse
```

```python
import jax
import jax.numpy as jnp
from jax import lax
from jax.experimental import pallas as pl
from jax.experimental.pallas import tpu as pltpu
from jax.sharding import PartitionSpec as P

F32 = jnp.float32
BF16 = jnp.bfloat16
MESH = pl.DeviceIdType.MESH
W = 128
NP = 8
RING = 4
PAIRS = 8
COLS = 2 * W


def split(value):
    high = value.astype(BF16)
    low = (value - high.astype(F32)).astype(BF16)
    return high, low


def kernel(
    a_hbm, lower_ref, structure_ref, pivot_ref, panel_hbm, diag_hbm,
    a_high, a_low, b_high, b_low, mask, gathered, partial,
    far, near, far_tile, near_tile, panel, correction,
    prow_in, prow_sum, x_in, y_in, diag,
    a_sem, out_sem, gather_send, gather_recv, scatter_send, scatter_recv,
    reduce_send, reduce_recv,
):
    prow, pcol = lax.axis_index("prow"), lax.axis_index("pcol")
    z, core = prow // 2, prow % 2
    x, y = pcol // RING, pcol % RING

    def along_x(step):
        return (prow, ((x + step) % RING) * RING + y)

    def along_y(step):
        return (prow, x * RING + (y + step) % RING)

    def along_prow(step):
        return ((prow + step) % NP, pcol)

    def tile_of(step, which):
        return ((z + step) % RING) * 2 + which

    sibling = (tile_of(0, 1 - core), pcol)
    z_next = (tile_of(1, core), pcol)
    z_last = (tile_of(3, core), pcol)

    def send(source, target, send_sem, recv_sem, device):
        pltpu.make_async_remote_copy(
            src_ref=source, dst_ref=target, send_sem=send_sem, recv_sem=recv_sem,
            device_id=device, device_id_type=MESH,
        ).start()

    def await_bytes(ref, sem):
        pltpu.make_async_copy(ref, ref, sem).wait()

    for part in range(8):
        pltpu.make_async_copy(a_hbm.at[part], partial.at[part], a_sem.at[part]).start()

    own = lower_ref[...]
    for pair in range(PAIRS):
        gathered[pair, prow] = own[:, pair * COLS:(pair + 1) * COLS]
    listed = jnp.where(structure_ref[...] == prow * 16 + pcol, 1.0, 0.0).astype(F32)
    mask[...] = jnp.broadcast_to(jnp.max(listed, axis=1, keepdims=True), mask.shape)

    barrier = pltpu.get_barrier_semaphore()
    partners = [along_prow(k) for k in range(1, NP)]
    partners += [along_x(k) for k in range(1, RING)]
    partners += [along_y(k) for k in range(1, RING)]
    for device in partners:
        pl.semaphore_signal(barrier, inc=1, device_id=device, device_id_type=MESH)
    pl.semaphore_wait(barrier, len(partners))

    def gather_send_to(t, ref, which, device):
        send(ref, ref, gather_send.at[t, which], gather_recv.at[t, which], device)

    half = W // 2

    def gather_first(t):
        ref = gathered.at[t, prow]
        gather_send_to(t, ref, 0, z_next)
        gather_send_to(t, ref, 1, z_last)
        gather_send_to(t, ref, 2, sibling)

    def gather_second(t):
        ref = gathered.at[t, tile_of(3, core)]
        await_bytes(ref, gather_recv.at[t, 0])
        gather_send_to(t, ref.at[pl.ds(0, half)], 5, z_next)
        gather_send_to(t, ref, 3, sibling)
        ref = gathered.at[t, tile_of(1, core)]
        await_bytes(ref, gather_recv.at[t, 1])
        gather_send_to(t, ref.at[pl.ds(half, half)], 6, z_last)
        gather_send_to(t, ref, 4, sibling)

    def gather_third(t):
        ref = gathered.at[t, tile_of(2, core)]
        await_bytes(ref.at[pl.ds(0, half)], gather_recv.at[t, 5])
        await_bytes(ref.at[pl.ds(half, half)], gather_recv.at[t, 6])
        gather_send_to(t, ref, 7, sibling)
        for which, step in ((2, 0), (3, 3), (4, 1), (7, 2)):
            await_bytes(gathered.at[t, tile_of(step, 1 - core)], gather_recv.at[t, which])

    def multiply(t):
        for tile in range(NP):
            high, low = split(gathered[t, tile])
            b_high[tile * W:(tile + 1) * W] = high
            b_low[tile * W:(tile + 1) * W] = low

        @pl.loop(0, RING)
        def _(i):
            rows = pl.ds(pl.multiple_of(i * 4 * W, 4 * W), 4 * W)
            total = jnp.dot(a_high[rows], b_high[...], preferred_element_type=F32)
            total += jnp.dot(a_low[rows], b_high[...], preferred_element_type=F32)
            total += jnp.dot(a_high[rows], b_low[...], preferred_element_type=F32)
            for j in range(RING):
                block = total[j * W:(j + 1) * W]
                partial[2 * t, i, j] = block[:, :W]
                partial[2 * t + 1, j, i] = block[:, W:]

    def routes(t):
        return (
            (2 * t, x, y, along_x, along_y),
            (2 * t + 1, y, x, along_y, along_x),
        )

    def scatter_send_to(b, which, source, target, device):
        send(source, target, scatter_send.at[b, which], scatter_recv.at[b, which], device)

    def scatter_first(t):
        for b, u, v, first, second in routes(t):
            block = partial.at[b, (u + 2) % RING]
            scatter_send_to(b, 0, block.at[pl.ds(0, 2)], far.at[b, 0], first(1))
            scatter_send_to(b, 1, block.at[pl.ds(2, 2)], far.at[b, 1], first(3))

    def scatter_second(t):
        for b, u, v, first, second in routes(t):
            up, down = (u + 1) % RING, (u + 3) % RING
            await_bytes(far.at[b, 0], scatter_recv.at[b, 0])
            partial[b, up, 0:2] += far[b, 0]
            scatter_send_to(b, 2, partial.at[b, up], near.at[b, 0], first(1))
            await_bytes(far.at[b, 1], scatter_recv.at[b, 1])
            partial[b, down, 2:4] += far[b, 1]
            scatter_send_to(b, 3, partial.at[b, down], near.at[b, 1], first(3))

    def scatter_third(t):
        for b, u, v, first, second in routes(t):
            await_bytes(near.at[b, 0], scatter_recv.at[b, 2])
            await_bytes(near.at[b, 1], scatter_recv.at[b, 3])
            partial[b, u] += near[b, 0] + near[b, 1]
            block = partial.at[b, u, (v + 2) % RING]
            scatter_send_to(b, 4, block.at[pl.ds(0, half)], far_tile.at[b, 0], second(1))
            scatter_send_to(b, 5, block.at[pl.ds(half, half)], far_tile.at[b, 1], second(3))

    def scatter_fourth(t):
        for b, u, v, first, second in routes(t):
            up, down = (v + 1) % RING, (v + 3) % RING
            await_bytes(far_tile.at[b, 0], scatter_recv.at[b, 4])
            partial[b, u, up, 0:half] += far_tile[b, 0]
            scatter_send_to(b, 6, partial.at[b, u, up], near_tile.at[b, 0], second(1))
            await_bytes(far_tile.at[b, 1], scatter_recv.at[b, 5])
            partial[b, u, down, half:W] += far_tile[b, 1]
            scatter_send_to(b, 7, partial.at[b, u, down], near_tile.at[b, 1], second(3))

    def columns(t):
        return pl.ds(pl.multiple_of(t * COLS, COLS), COLS)

    def finish(t):
        for h, (b, u, v, first, second) in enumerate(routes(t)):
            await_bytes(near_tile.at[b, 0], scatter_recv.at[b, 6])
            await_bytes(near_tile.at[b, 1], scatter_recv.at[b, 7])
            product = partial[b, u, v] + near_tile[b, 0] + near_tile[b, 1]
            block = -(product * mask[pl.ds(b, 1), :])
            panel[t, :, h * W:(h + 1) * W] = block
            correction[t, h * W:(h + 1) * W] = lax.dot_general(
                gathered[t, prow, :, h * W:(h + 1) * W], block,
                (((0,), (0,)), ((), ())),
                precision=lax.Precision.HIGHEST, preferred_element_type=F32,
            )
        pltpu.make_async_copy(panel.at[t], panel_hbm.at[:, columns(t)], out_sem.at[0, t]).start()
        for k in range(1, NP):
            rows = pl.ds(pl.multiple_of(((prow + k) % NP) * 32, 32), 32)
            send(correction.at[t, rows], prow_in.at[t, k],
                 reduce_send.at[t, 0], reduce_recv.at[t, 0], along_prow(k))

    own_rows = pl.ds(pl.multiple_of(prow * 32, 32), 32)
    final_rows = pl.ds(pl.multiple_of(prow * 32 + x * 8, 8), 8)

    def reduce_second(t):
        await_bytes(prow_in.at[t, pl.ds(1, NP - 1)], reduce_recv.at[t, 0])
        total = correction[t, own_rows]
        for k in range(1, NP):
            total += prow_in[t, k]
        prow_sum[t] = total
        for k in range(1, RING):
            rows = pl.ds(pl.multiple_of(((x + k) % RING) * 8, 8), 8)
            send(prow_sum.at[t, rows], x_in.at[t, k],
                 reduce_send.at[t, 1], reduce_recv.at[t, 1], along_x(k))

    def reduce_third(t):
        await_bytes(x_in.at[t, pl.ds(1, RING - 1)], reduce_recv.at[t, 1])
        total = prow_sum[t, pl.ds(pl.multiple_of(x * 8, 8), 8)]
        for k in range(1, RING):
            total += x_in[t, k]
        y_in[t, y] = total
        for k in range(1, RING):
            send(y_in.at[t, y], y_in.at[t, y],
                 reduce_send.at[t, 2], reduce_recv.at[t, 2], along_y(k))

    def reduce_fourth(t):
        await_bytes(y_in.at[t, pl.ds(0, RING - 1)], reduce_recv.at[t, 2])
        total = (y_in[t, 0] + y_in[t, 1]) + (y_in[t, 2] + y_in[t, 3])
        rows = pl.ds(pl.multiple_of(t * COLS + prow * 32 + x * 8, 8), 8)
        diag[t, final_rows] = pivot_ref[rows] - total
        for k in range(1, RING):
            send(diag.at[t, final_rows], diag.at[t, final_rows],
                 reduce_send.at[t, 3], reduce_recv.at[t, 3], along_x(k))

    def reduce_fifth(t):
        await_bytes(diag.at[t, pl.ds(0, 24)], reduce_recv.at[t, 3])
        for k in range(1, NP):
            send(diag.at[t, own_rows], diag.at[t, own_rows],
                 reduce_send.at[t, 4], reduce_recv.at[t, 4], along_prow(k))

    def reduce_last(t):
        await_bytes(diag.at[t, pl.ds(0, 224)], reduce_recv.at[t, 4])
        rows = pl.ds(pl.multiple_of(t * COLS, COLS), COLS)
        pltpu.make_async_copy(diag.at[t], diag_hbm.at[rows], out_sem.at[1, t]).start()

    gather_first(0)

    for part in range(8):
        await_bytes(partial.at[part], a_sem.at[part])

        @pl.loop(0, 16)
        def _(i):
            rows = pl.ds(pl.multiple_of(part * 256 + i * 16, 16), 16)
            for r in range(NP):
                high, low = split(partial[part, i // 4, i % 4, pl.ds(r, 16, stride=8), :])
                a_high[rows, r * W:(r + 1) * W] = high
                a_low[rows, r * W:(r + 1) * W] = low

    @pl.loop(0, 20)
    def _(step):
        def at(lag, body):
            t = step - lag

            @pl.when((t >= 0) & (t < PAIRS))
            def _():
                body(t)

        at(4, scatter_second)
        at(5, scatter_third)
        at(6, scatter_fourth)
        at(7, finish)
        at(8, reduce_second)
        at(9, reduce_third)
        at(10, reduce_fourth)
        at(11, reduce_fifth)
        at(12, reduce_last)
        at(2, gather_third)
        at(2, multiply)
        at(2, scatter_first)
        at(1, gather_second)

        @pl.when(step + 1 < PAIRS)
        def _():
            gather_first(step + 1)

    @pl.loop(0, PAIRS)
    def _(t):
        for which in range(8):
            ref = gathered.at[t, 0]
            await_bytes(ref.at[pl.ds(0, half)] if which in (5, 6) else ref, gather_send.at[t, which])
        for b in (2 * t, 2 * t + 1):
            for which in range(8):
                buffer = (far, near, far_tile, near_tile)[which // 2]
                await_bytes(buffer.at[b, which % 2], scatter_send.at[b, which])
        await_bytes(prow_in.at[t, pl.ds(1, NP - 1)], reduce_send.at[t, 0])
        await_bytes(x_in.at[t, pl.ds(1, RING - 1)], reduce_send.at[t, 1])
        await_bytes(y_in.at[t, pl.ds(0, RING - 1)], reduce_send.at[t, 2])
        await_bytes(diag.at[t, pl.ds(0, 24)], reduce_send.at[t, 3])
        await_bytes(diag.at[t, pl.ds(0, 224)], reduce_send.at[t, 4])
        await_bytes(panel.at[t], out_sem.at[0, t])
        await_bytes(diag.at[t], out_sem.at[1, t])


def on_device(ancestor_inverse, lower_panel, structure, pivot_inverse):
    rows = ancestor_inverse.shape[0]
    blocks = ancestor_inverse.reshape(8, 4, 4, W, W)
    pivot_rows = pivot_inverse.reshape(16 * W, W)
    vmem = pl.BlockSpec(memory_space=pltpu.VMEM)
    hbm = pl.BlockSpec(memory_space=pl.ANY)
    depth = NP * W
    dma = pltpu.SemaphoreType.DMA
    panel, diag = pl.pallas_call(
        kernel,
        out_shape=(
            jax.ShapeDtypeStruct(lower_panel.shape, F32),
            jax.ShapeDtypeStruct(pivot_rows.shape, F32),
        ),
        in_specs=[hbm, vmem, vmem, vmem],
        out_specs=(hbm, hbm),
        scratch_shapes=[
            pltpu.VMEM((rows, depth), BF16),
            pltpu.VMEM((rows, depth), BF16),
            pltpu.VMEM((depth, COLS), BF16),
            pltpu.VMEM((depth, COLS), BF16),
            pltpu.VMEM((16, W), F32),
            pltpu.VMEM((PAIRS, NP, W, COLS), F32),
            pltpu.VMEM((16, RING, RING, W, W), F32),
            pltpu.VMEM((16, 2, 2, W, W), F32),
            pltpu.VMEM((16, 2, 4, W, W), F32),
            pltpu.VMEM((16, 2, W // 2, W), F32),
            pltpu.VMEM((16, 2, W, W), F32),
            pltpu.VMEM((PAIRS, W, COLS), F32),
            pltpu.VMEM((PAIRS, COLS, W), F32),
            pltpu.VMEM((PAIRS, NP, 32, W), F32),
            pltpu.VMEM((PAIRS, 32, W), F32),
            pltpu.VMEM((PAIRS, RING, 8, W), F32),
            pltpu.VMEM((PAIRS, RING, 8, W), F32),
            pltpu.VMEM((PAIRS, COLS, W), F32),
            dma((8,)),
            dma((2, PAIRS)),
            dma((PAIRS, 8)),
            dma((PAIRS, 8)),
            dma((16, 8)),
            dma((16, 8)),
            dma((PAIRS, 5)),
            dma((PAIRS, 5)),
        ],
        compiler_params=pltpu.CompilerParams(
            collective_id=0, has_side_effects=True, vmem_limit_bytes=62 * 1024 * 1024,
        ),
        cost_estimate=pl.CostEstimate(
            flops=2 * 3 * rows * depth * lower_panel.shape[1], bytes_accessed=12 << 20, transcendentals=0,
        ),
    )(blocks, lower_panel, structure, pivot_rows)
    return panel, diag.reshape(pivot_inverse.shape)


def solution(mesh):
    return jax.shard_map(
        on_device,
        mesh=mesh,
        in_specs=(P("prow", None, "pcol", None), P(("prow", "pcol"), None), P(), P()),
        out_specs=(P(("prow", "pcol"), None), P()),
        check_vma=False,
    )
```

```python
import jax
import jax.numpy as jnp
from jax import lax
from jax.experimental import pallas as pl
from jax.experimental.pallas import tpu as pltpu
from jax.sharding import PartitionSpec as P

F32 = jnp.float32
BF16 = jnp.bfloat16
MESH = pl.DeviceIdType.MESH
W = 128
HALF = W // 2
NP = 8
RING = 4
PAIRS = 8
LAST = PAIRS - 1
COLS = 2 * W
EARLY = 2
LATE = 2
MIDDLE = 4


def split(value):
    high = value.astype(BF16)
    low = (value - high.astype(F32)).astype(BF16)
    return high, low


def aligned(start, size):
    return pl.ds(pl.multiple_of(start, size), size)


def kernel(
    a_hbm, lower_hbm, structure_ref, pivot_hbm, panel_hbm, diag_hbm,
    a_high, a_low, b_high, b_low, mask, ring_mask, gathered, partial,
    far, near, far_tile, near_tile, panel, correction, ring_lower, ring_panel,
    prow_in, x_in, y_in, pivot, diag,
    a_sem, lower_sem, pivot_sem, out_sem, gather_send, gather_recv,
    scatter_send, scatter_recv, reduce_send, reduce_recv, ring_sem,
):
    prow, pcol = lax.axis_index("prow"), lax.axis_index("pcol")
    z, core = prow // 2, prow % 2
    x, y = pcol // RING, pcol % RING

    def along_x(step):
        return (prow, ((x + step) % RING) * RING + y)

    def along_y(step):
        return (prow, x * RING + (y + step) % RING)

    def along_prow(step):
        return ((prow + step) % NP, pcol)

    def tile_of(step, which):
        return ((z + step) % RING) * 2 + which

    sibling = (tile_of(0, 1 - core), pcol)
    z_next = (tile_of(1, core), pcol)
    z_last = (tile_of(3, core), pcol)

    def send(source, target, send_sem, recv_sem, device):
        pltpu.make_async_remote_copy(
            src_ref=source, dst_ref=target, send_sem=send_sem, recv_sem=recv_sem,
            device_id=device, device_id_type=MESH,
        ).start()

    def await_bytes(ref, sem):
        pltpu.make_async_copy(ref, ref, sem).wait()

    barrier = pltpu.get_barrier_semaphore()
    partners = [along_prow(k) for k in range(1, NP)]
    partners += [along_x(k) for k in range(1, RING)]
    partners += [along_y(k) for k in range(1, RING)]
    for device in partners:
        pl.semaphore_signal(barrier, inc=1, device_id=device, device_id_type=MESH)

    for t in range(PAIRS):
        pltpu.make_async_copy(
            lower_hbm.at[:, pl.ds(t * COLS, COLS)], gathered.at[t, prow], lower_sem.at[min(t, 1)]
        ).start()
    for part in range(4):
        pltpu.make_async_copy(
            a_hbm.at[pl.ds(2 * part, 2)], partial.at[pl.ds(2 * part, 2)], a_sem.at[part]
        ).start()
    own_rows = aligned(prow * 32, 32)
    pltpu.make_async_copy(pivot_hbm.at[:, own_rows], pivot, pivot_sem).start()

    def member(tile):
        listed = jnp.where(structure_ref[...] == prow * 16 + tile, 1.0, 0.0).astype(F32)
        return jnp.broadcast_to(jnp.max(listed, axis=1, keepdims=True), mask.shape)

    mask[...] = member(pcol)
    for k in range(RING):
        ring_mask[0, k] = member(x * RING + k)
        ring_mask[1, k] = member(k * RING + y)

    await_bytes(gathered.at[0, prow], lower_sem.at[0])
    pl.semaphore_wait(barrier, len(partners))

    def gather_send_to(t, ref, which, recv, device):
        send(ref, ref, gather_send.at[which], recv, device)

    def gather_first(t):
        ref = gathered.at[t, prow]
        gather_send_to(t, ref, 0, gather_recv.at[t, 0], z_next)
        gather_send_to(t, ref, 1, gather_recv.at[t, 1], z_last)
        gather_send_to(t, ref, 2, gather_recv.at[t, 3], sibling)

    def gather_second(t):
        ref = gathered.at[t, tile_of(3, core)]
        await_bytes(ref, gather_recv.at[t, 0])
        gather_send_to(t, ref.at[pl.ds(0, HALF)], 5, gather_recv.at[t, 2], z_next)
        gather_send_to(t, ref, 3, gather_recv.at[t, 4], sibling)
        ref = gathered.at[t, tile_of(1, core)]
        await_bytes(ref, gather_recv.at[t, 1])
        gather_send_to(t, ref.at[pl.ds(HALF, HALF)], 6, gather_recv.at[t, 2], z_last)
        gather_send_to(t, ref, 4, gather_recv.at[t, 5], sibling)

    def gather_third(t):
        ref = gathered.at[t, tile_of(2, core)]
        await_bytes(ref, gather_recv.at[t, 2])
        gather_send_to(t, ref, 7, gather_recv.at[t, 6], sibling)

    def gather_wait(t):
        for k, step in enumerate((0, 3, 1, 2)):
            await_bytes(gathered.at[t, tile_of(step, 1 - core)], gather_recv.at[t, 3 + k])

    def multiply(t):
        for tile in range(NP):
            high, low = split(gathered[t, tile])
            b_high[tile * W:(tile + 1) * W] = high
            b_low[tile * W:(tile + 1) * W] = low

        @pl.loop(0, RING)
        def _(i):
            rows = aligned(i * 4 * W, 4 * W)
            total = jnp.dot(a_high[rows], b_high[...], preferred_element_type=F32)
            total += jnp.dot(a_low[rows], b_high[...], preferred_element_type=F32)
            total += jnp.dot(a_high[rows], b_low[...], preferred_element_type=F32)
            for j in range(RING):
                block = total[j * W:(j + 1) * W]
                partial[2 * t, i, j] = block[:, :W]
                partial[2 * t + 1, j, i] = block[:, W:]

    def multiply_first():
        @pl.loop(0, RING)
        def _(k):
            step = jnp.where(k == 0, 0, jnp.where(k == 1, 3, jnp.where(k == 2, 1, 2)))

            @pl.when(k == 3)
            def _():
                gather_third(0)

            chip = (z + step) % RING
            depth = aligned(chip * COLS, COLS)
            await_bytes(gathered.at[0, chip * 2 + 1 - core], gather_recv.at[0, 3 + k])
            for which in range(2):
                high, low = split(gathered[0, chip * 2 + which])
                b_high[which * W:(which + 1) * W] = high
                b_low[which * W:(which + 1) * W] = low

            @pl.loop(0, RING)
            def _(i):
                rows = aligned(i * 4 * W, 4 * W)
                high, low = b_high[0:COLS], b_low[0:COLS]
                total = jnp.dot(a_high[rows, depth], high, preferred_element_type=F32)
                total += jnp.dot(a_low[rows, depth], high, preferred_element_type=F32)
                total += jnp.dot(a_high[rows, depth], low, preferred_element_type=F32)
                for j in range(RING):
                    block = total[j * W:(j + 1) * W]
                    partial[0, i, j] = block[:, :W] + jnp.where(k == 0, 0.0, partial[0, i, j])
                    partial[1, j, i] = block[:, W:] + jnp.where(k == 0, 0.0, partial[1, j, i])

    def routes(t):
        return (
            (2 * t, x, y, along_x, along_y),
            (2 * t + 1, y, x, along_y, along_x),
        )

    def scatter_send_to(t, which, source, target, device):
        send(source, target, scatter_send.at[which], scatter_recv.at[t, which // 2], device)

    def scatter_first(t):
        for b, u, v, first, second in routes(t):
            block = partial.at[b, (u + 2) % RING]
            scatter_send_to(t, 0, block.at[pl.ds(0, 2)], far.at[b, 0], first(1))
            scatter_send_to(t, 1, block.at[pl.ds(2, 2)], far.at[b, 1], first(3))

    def scatter_second(t):
        await_bytes(far.at[pl.ds(2 * t, 2)], scatter_recv.at[t, 0])
        for b, u, v, first, second in routes(t):
            up, down = (u + 1) % RING, (u + 3) % RING
            partial[b, up, 0:2] += far[b, 0]
            scatter_send_to(t, 2, partial.at[b, up], near.at[b, 0], first(1))
            partial[b, down, 2:4] += far[b, 1]
            scatter_send_to(t, 3, partial.at[b, down], near.at[b, 1], first(3))

    def scatter_third(t):
        await_bytes(near.at[pl.ds(2 * t, 2)], scatter_recv.at[t, 1])
        for b, u, v, first, second in routes(t):
            partial[b, u] += near[b, 0] + near[b, 1]

    def scatter_turn(t):
        for b, u, v, first, second in routes(t):
            block = partial.at[b, u, (v + 2) % RING]
            scatter_send_to(t, 4, block.at[pl.ds(0, HALF)], far_tile.at[b, 0], second(1))
            scatter_send_to(t, 5, block.at[pl.ds(HALF, HALF)], far_tile.at[b, 1], second(3))

    def scatter_fourth(t):
        await_bytes(far_tile.at[pl.ds(2 * t, 2)], scatter_recv.at[t, 2])
        for b, u, v, first, second in routes(t):
            up, down = (v + 1) % RING, (v + 3) % RING
            partial[b, u, up, 0:HALF] += far_tile[b, 0]
            scatter_send_to(t, 6, partial.at[b, u, up], near_tile.at[b, 0], second(1))
            partial[b, u, down, HALF:W] += far_tile[b, 1]
            scatter_send_to(t, 7, partial.at[b, u, down], near_tile.at[b, 1], second(3))

    def finish(t):
        await_bytes(near_tile.at[pl.ds(2 * t, 2)], scatter_recv.at[t, 3])
        for h, (b, u, v, first, second) in enumerate(routes(t)):
            product = partial[b, u, v] + near_tile[b, 0] + near_tile[b, 1]
            panel[t, :, h * W:(h + 1) * W] = -(product * mask[pl.ds(b, 1), :])
        columns = aligned(t * COLS, COLS)
        pltpu.make_async_copy(panel.at[t], panel_hbm.at[:, columns], out_sem.at[0]).start()

    def correct(t):
        for h in range(2):
            correction[t, h * W:(h + 1) * W] = lax.dot_general(
                gathered[t, prow, :, h * W:(h + 1) * W], panel[t, :, h * W:(h + 1) * W],
                (((0,), (0,)), ((), ())),
                precision=lax.Precision.HIGHEST, preferred_element_type=F32,
            )

    def ring_send():
        for t in range(EARLY, PAIRS):
            for h, (step, slot) in enumerate(((along_y, y), (along_x, x))):
                source = gathered.at[t, prow, :, pl.ds(h * W, W)]
                ring_lower[t - EARLY, h, slot] = source[...]
                for k in range(1, RING):
                    send(source, ring_lower.at[t - EARLY, h, slot], ring_sem.at[0], ring_sem.at[1], step(k))

    def correct_early(t):
        for h, (b, u, v, first, second) in enumerate(routes(t)):
            for k in range(RING):
                ring_panel[k] = -(partial[b, u, k] * ring_mask[h, k, pl.ds(b, 1), :])
            correction[t, h * W:(h + 1) * W] = lax.dot_general(
                ring_lower[t - EARLY, h].reshape(RING * W, W), ring_panel[...].reshape(RING * W, W),
                (((0,), (0,)), ((), ())),
                precision=lax.Precision.HIGHEST, preferred_element_type=F32,
            )

    def reduce_send_to(t, stage, source, target, device):
        send(source, target, reduce_send.at[stage], reduce_recv.at[t, stage], device)

    def reduce_first(t):
        for k in range(1, NP):
            rows = aligned(((prow + k) % NP) * 32, 32)
            reduce_send_to(t, 0, correction.at[t, rows], prow_in.at[k, t], along_prow(k))

    def reduce_second(t):
        await_bytes(prow_in.at[pl.ds(1, NP - 1), t], reduce_recv.at[t, 0])
        total = correction[t, own_rows]
        for k in range(1, NP):
            total += prow_in[k, t]
        x_in[x, t] = total
        for k in range(1, RING):
            ref = x_in.at[x, t]
            reduce_send_to(t, 1, ref, ref, along_x(k))

    def reduce_third(t):
        await_bytes(x_in.at[pl.ds(0, RING - 1), t], reduce_recv.at[t, 1])
        y_in[y, t] = (x_in[0, t] + x_in[1, t]) + (x_in[2, t] + x_in[3, t])
        for k in range(1, RING):
            ref = y_in.at[y, t]
            reduce_send_to(t, 2, ref, ref, along_y(k))

    def reduce_fourth(t):
        await_bytes(y_in.at[pl.ds(0, RING - 1), t], reduce_recv.at[t, 2])
        total = (y_in[0, t] + y_in[1, t]) + (y_in[2, t] + y_in[3, t])
        diag[t, own_rows] = pivot[t] - total
        for k in range(1, NP):
            ref = diag.at[t, own_rows]
            reduce_send_to(t, 3, ref, ref, along_prow(k))

    def reduce_last(t):
        await_bytes(diag.at[t, pl.ds(0, 224)], reduce_recv.at[t, 3])
        pltpu.make_async_copy(diag.at[t], diag_hbm.at[t], out_sem.at[1]).start()

    def prepare():
        await_bytes(gathered.at[pl.ds(1, PAIRS - 1), prow], lower_sem.at[1])
        ring_send()

        @pl.loop(0, 128)
        def _(i):
            part = i // 32

            @pl.when(i % 32 == 0)
            def _():
                await_bytes(partial.at[pl.ds(2 * part, 2)], a_sem.at[part])

            rows = aligned(i * 16, 16)
            for r in range(NP):
                high, low = split(partial[i // 16, (i // 4) % 4, i % 4, pl.ds(r, 16, stride=8), :])
                a_high[rows, r * W:(r + 1) * W] = high
                a_low[rows, r * W:(r + 1) * W] = low

        await_bytes(pivot, pivot_sem)

    @pl.loop(-2, PAIRS + 7)
    def _(step):
        def at(lag, body, first=0, end=PAIRS):
            t = step - lag

            @pl.when((t >= first) & (t < end))
            def _():
                body(t)

        def once(when, body, *args):
            @pl.when(step == when)
            def _():
                body(*args)

        def late(when, body, first=LATE, end=PAIRS):
            @pl.when(step == when)
            def _():
                @pl.loop(first, end)
                def _(t):
                    body(t)

        at(9, reduce_last, 0, EARLY)
        at(8, reduce_fourth, 0, EARLY)
        at(7, reduce_third, 0, EARLY)
        at(6, reduce_second, 0, EARLY)
        late(LAST + 6, finish, LATE, MIDDLE)
        at(7, reduce_last, EARLY)
        at(6, reduce_fourth, EARLY)
        at(5, reduce_third, EARLY)
        at(4, reduce_second, EARLY)
        late(LAST + 4, scatter_fourth, LATE, MIDDLE)
        late(LAST + 5, scatter_fourth, MIDDLE, PAIRS)
        late(LAST + 6, finish, MIDDLE, PAIRS)
        at(2, scatter_second)
        once(EARLY + 3, await_bytes, ring_lower.at[:, :, pl.ds(0, RING - 1)], ring_sem.at[1])
        late(LAST + 3, scatter_turn, LATE, LAST)
        at(3, scatter_third)
        at(3, scatter_turn, 0, LATE)
        at(3, scatter_turn, LAST)
        at(3, correct_early, EARLY)
        at(3, reduce_first, EARLY)
        at(4, scatter_fourth, 0, LATE)
        at(5, finish, 0, LATE)
        at(5, correct, 0, EARLY)
        at(5, reduce_first, 0, EARLY)
        once(0, multiply_first)
        at(0, gather_third, 1)
        at(0, gather_wait, 1)
        at(0, multiply, 1)
        at(0, scatter_first)
        once(-1, prepare)
        at(-1, gather_second)
        at(-2, gather_first)

    for which in range(8):
        ref = gathered.at[:, 0]
        await_bytes(ref.at[:, pl.ds(0, HALF)] if which in (5, 6) else ref, gather_send.at[which])
        buffer = (far, near, far_tile, near_tile)[which // 2]
        await_bytes(buffer.at[:, which % 2], scatter_send.at[which])
    await_bytes(ring_lower.at[:, :, pl.ds(0, RING - 1)], ring_sem.at[0])
    await_bytes(prow_in.at[pl.ds(1, NP - 1)], reduce_send.at[0])
    await_bytes(x_in.at[pl.ds(0, RING - 1)], reduce_send.at[1])
    await_bytes(y_in.at[pl.ds(0, RING - 1)], reduce_send.at[2])
    await_bytes(diag.at[:, pl.ds(0, 224)], reduce_send.at[3])
    await_bytes(panel, out_sem.at[0])
    await_bytes(diag, out_sem.at[1])


def hand_over(panel_in, diag_in, panel_out, diag_out, panel_space, diag_space, sem):
    def parts(panel, diag):
        for k in range(4):
            yield panel.at[pl.ds(k * W // 4, W // 4)]
            yield diag.at[pl.ds(k * 2, 2)]

    stages = [list(parts(*refs)) for refs in (
        (panel_in, diag_in), (panel_space, diag_space), (panel_out, diag_out))]
    loads, stores = (
        [pltpu.make_async_copy(a, b, sem.at[n, k]) for k, (a, b) in enumerate(zip(*stages[n:n + 2]))]
        for n in range(2)
    )
    for load in loads:
        load.start()
    for load, store in zip(loads, stores):
        load.wait()
        store.start()
    for store in stores:
        store.wait()


def on_device(ancestor_inverse, lower_panel, structure, pivot_inverse):
    rows = ancestor_inverse.shape[0]
    blocks = ancestor_inverse.reshape(8, 4, 4, W, W)
    pivot_pairs = pivot_inverse.reshape(PAIRS, COLS, W)
    vmem = pl.BlockSpec(memory_space=pltpu.VMEM)
    hbm = pl.BlockSpec(memory_space=pl.ANY)
    depth = NP * W
    dma = pltpu.SemaphoreType.DMA
    out_shape = (
        jax.ShapeDtypeStruct(lower_panel.shape, F32),
        jax.ShapeDtypeStruct(pivot_pairs.shape, F32),
    )
    panel, diag = pl.pallas_call(
        kernel,
        out_shape=out_shape,
        in_specs=[hbm, hbm, vmem, hbm],
        out_specs=(hbm, hbm),
        scratch_shapes=[
            pltpu.VMEM((rows, depth), BF16),
            pltpu.VMEM((rows, depth), BF16),
            pltpu.VMEM((depth, COLS), BF16),
            pltpu.VMEM((depth, COLS), BF16),
            pltpu.VMEM((16, W), F32),
            pltpu.VMEM((2, RING, 16, W), F32),
            pltpu.VMEM((PAIRS, NP, W, COLS), F32),
            pltpu.VMEM((16, RING, RING, W, W), F32),
            pltpu.VMEM((16, 2, 2, W, W), F32),
            pltpu.VMEM((16, 2, 4, W, W), F32),
            pltpu.VMEM((16, 2, HALF, W), F32),
            pltpu.VMEM((16, 2, W, W), F32),
            pltpu.VMEM((PAIRS, W, COLS), F32),
            pltpu.VMEM((PAIRS, COLS, W), F32),
            pltpu.VMEM((PAIRS - EARLY, 2, RING, W, W), F32),
            pltpu.VMEM((RING, W, W), F32),
            pltpu.VMEM((NP, PAIRS, 32, W), F32),
            pltpu.VMEM((RING, PAIRS, 32, W), F32),
            pltpu.VMEM((RING, PAIRS, 32, W), F32),
            pltpu.VMEM((PAIRS, 32, W), F32),
            pltpu.VMEM((PAIRS, COLS, W), F32),
            dma((4,)),
            dma((2,)),
            dma,
            dma((2,)),
            dma((8,)),
            dma((PAIRS, 7)),
            dma((8,)),
            dma((PAIRS, 4)),
            dma((4,)),
            dma((PAIRS, 4)),
            dma((2,)),
        ],
        compiler_params=pltpu.CompilerParams(
            collective_id=0, has_side_effects=True, vmem_limit_bytes=62 * 1024 * 1024,
        ),
        cost_estimate=pl.CostEstimate(
            flops=2 * 3 * rows * depth * lower_panel.shape[1], bytes_accessed=12 << 20, transcendentals=0,
        ),
    )(blocks, lower_panel, structure, pivot_pairs)
    panel, diag = pl.pallas_call(
        hand_over,
        out_shape=out_shape,
        in_specs=[hbm, hbm],
        out_specs=(hbm, hbm),
        scratch_shapes=[
            pltpu.VMEM(out_shape[0].shape, F32), pltpu.VMEM(out_shape[1].shape, F32), dma((2, 8)),
        ],
        compiler_params=pltpu.CompilerParams(vmem_limit_bytes=62 * 1024 * 1024),
    )(panel, diag)
    return panel, diag.reshape(pivot_inverse.shape)


def solution(mesh):
    return jax.shard_map(
        on_device,
        mesh=mesh,
        in_specs=(P("prow", None, "pcol", None), P(("prow", "pcol"), None), P(), P()),
        out_specs=(P(("prow", "pcol"), None), P()),
        check_vma=False,
    )
```

```python
import jax
import jax.numpy as jnp
from jax import lax
from jax.experimental import pallas as pl
from jax.experimental.pallas import tpu as pltpu
from jax.sharding import PartitionSpec as P

F32 = jnp.float32
BF16 = jnp.bfloat16
MESH = pl.DeviceIdType.MESH
W = 128
HALF = W // 2
NP = 8
RING = 4
PAIRS = 8
LAST = PAIRS - 1
COLS = 2 * W
EARLY = 2
LATE = 2
MIDDLE = 4


def split(value):
    high = value.astype(BF16)
    low = (value - high.astype(F32)).astype(BF16)
    return high, low


def aligned(start, size):
    return pl.ds(pl.multiple_of(start, size), size)


def kernel(
    a_hbm, lower_hbm, structure_ref, pivot_hbm, panel_hbm, diag_hbm,
    a_high, a_low, b_high, b_low, mask, ring_mask, gathered, partial,
    far, near, far_tile, near_tile, panel, correction, ring_lower, ring_panel,
    prow_in, x_in, y_in, pivot, diag,
    a_sem, lower_sem, pivot_sem, out_sem, gather_send, gather_recv,
    scatter_send, scatter_recv, reduce_send, reduce_recv, ring_sem,
):
    prow, pcol = lax.axis_index("prow"), lax.axis_index("pcol")
    z, core = prow // 2, prow % 2
    x, y = pcol // RING, pcol % RING

    def along_x(step):
        return (prow, ((x + step) % RING) * RING + y)

    def along_y(step):
        return (prow, x * RING + (y + step) % RING)

    def along_prow(step):
        return ((prow + step) % NP, pcol)

    def tile_of(step, which):
        return ((z + step) % RING) * 2 + which

    sibling = (tile_of(0, 1 - core), pcol)
    z_next = (tile_of(1, core), pcol)
    z_last = (tile_of(3, core), pcol)

    def send(source, target, send_sem, recv_sem, device):
        pltpu.make_async_remote_copy(
            src_ref=source, dst_ref=target, send_sem=send_sem, recv_sem=recv_sem,
            device_id=device, device_id_type=MESH,
        ).start()

    def await_bytes(ref, sem):
        pltpu.make_async_copy(ref, ref, sem).wait()

    barrier = pltpu.get_barrier_semaphore()
    partners = [along_prow(k) for k in range(1, NP)]
    partners += [along_x(k) for k in range(1, RING)]
    partners += [along_y(k) for k in range(1, RING)]
    for device in partners:
        pl.semaphore_signal(barrier, inc=1, device_id=device, device_id_type=MESH)

    for t in range(PAIRS):
        pltpu.make_async_copy(
            lower_hbm.at[:, pl.ds(t * COLS, COLS)], gathered.at[t, prow], lower_sem.at[min(t, 1)]
        ).start()
    for part in range(4):
        pltpu.make_async_copy(
            a_hbm.at[pl.ds(2 * part, 2)], partial.at[pl.ds(2 * part, 2)], a_sem.at[part]
        ).start()
    own_rows = aligned(prow * 32, 32)
    pltpu.make_async_copy(pivot_hbm.at[:, own_rows], pivot, pivot_sem).start()

    def member(tile):
        listed = jnp.where(structure_ref[...] == prow * 16 + tile, 1.0, 0.0).astype(F32)
        return jnp.broadcast_to(jnp.max(listed, axis=1, keepdims=True), mask.shape)

    mask[...] = member(pcol)
    for k in range(RING):
        ring_mask[0, k] = member(x * RING + k)
        ring_mask[1, k] = member(k * RING + y)

    await_bytes(gathered.at[0, prow], lower_sem.at[0])
    pl.semaphore_wait(barrier, len(partners))

    def gather_send_to(t, ref, which, recv, device):
        send(ref, ref, gather_send.at[which], recv, device)

    def gather_first(t):
        ref = gathered.at[t, prow]
        gather_send_to(t, ref, 0, gather_recv.at[t, 0], z_next)
        gather_send_to(t, ref, 1, gather_recv.at[t, 1], z_last)
        gather_send_to(t, ref, 2, gather_recv.at[t, 3], sibling)

    def gather_second(t):
        ref = gathered.at[t, tile_of(3, core)]
        await_bytes(ref, gather_recv.at[t, 0])
        gather_send_to(t, ref.at[pl.ds(0, HALF)], 5, gather_recv.at[t, 2], z_next)
        gather_send_to(t, ref, 3, gather_recv.at[t, 4], sibling)
        ref = gathered.at[t, tile_of(1, core)]
        await_bytes(ref, gather_recv.at[t, 1])
        gather_send_to(t, ref.at[pl.ds(HALF, HALF)], 6, gather_recv.at[t, 2], z_last)
        gather_send_to(t, ref, 4, gather_recv.at[t, 5], sibling)

    def gather_third(t):
        ref = gathered.at[t, tile_of(2, core)]
        await_bytes(ref, gather_recv.at[t, 2])
        gather_send_to(t, ref, 7, gather_recv.at[t, 6], sibling)

    def gather_wait(t):
        for k, step in enumerate((0, 3, 1, 2)):
            await_bytes(gathered.at[t, tile_of(step, 1 - core)], gather_recv.at[t, 3 + k])

    def multiply(t):
        for tile in range(NP):
            high, low = split(gathered[t, tile])
            b_high[tile * W:(tile + 1) * W] = high
            b_low[tile * W:(tile + 1) * W] = low

    def multiply_rows(h):
        def body(t):
            rows = pl.ds(h * 8 * W, 8 * W)
            total = jnp.dot(a_high[rows], b_high[...], preferred_element_type=F32)
            total += jnp.dot(a_low[rows], b_high[...], preferred_element_type=F32)
            total += jnp.dot(a_high[rows], b_low[...], preferred_element_type=F32)
            for n in range(8):
                i, j = h * 2 + n // 4, n % 4
                block = total[n * W:(n + 1) * W]
                partial[2 * t, i, j] = block[:, :W]
                partial[2 * t + 1, j, i] = block[:, W:]
        return body

    def multiply_first():
        @pl.loop(0, RING)
        def _(k):
            step = jnp.where(k == 0, 0, jnp.where(k == 1, 3, jnp.where(k == 2, 1, 2)))

            @pl.when(k == 3)
            def _():
                gather_third(0)

            chip = (z + step) % RING
            depth = aligned(chip * COLS, COLS)
            await_bytes(gathered.at[0, chip * 2 + 1 - core], gather_recv.at[0, 3 + k])
            for which in range(2):
                high, low = split(gathered[0, chip * 2 + which])
                b_high[which * W:(which + 1) * W] = high
                b_low[which * W:(which + 1) * W] = low

            high, low = b_high[0:COLS], b_low[0:COLS]

            @pl.loop(0, 2)
            def _(h):
                rows = aligned(h * 8 * W, 8 * W)
                total = jnp.dot(a_high[rows, depth], high, preferred_element_type=F32)
                total += jnp.dot(a_low[rows, depth], high, preferred_element_type=F32)
                total += jnp.dot(a_high[rows, depth], low, preferred_element_type=F32)
                for n in range(8):
                    i, j = h * 2 + n // 4, n % 4
                    block = total[n * W:(n + 1) * W]
                    partial[0, i, j] = block[:, :W] + jnp.where(k == 0, 0.0, partial[0, i, j])
                    partial[1, j, i] = block[:, W:] + jnp.where(k == 0, 0.0, partial[1, j, i])

    def routes(t):
        return (
            (2 * t, x, y, along_x, along_y),
            (2 * t + 1, y, x, along_y, along_x),
        )

    def scatter_send_to(t, which, source, target, device):
        send(source, target, scatter_send.at[which], scatter_recv.at[t, which // 2], device)

    def scatter_first(t):
        for b, u, v, first, second in routes(t):
            block = partial.at[b, (u + 2) % RING]
            scatter_send_to(t, 0, block.at[pl.ds(0, 2)], far.at[b, 0], first(1))
            scatter_send_to(t, 1, block.at[pl.ds(2, 2)], far.at[b, 1], first(3))

    def scatter_second(t):
        await_bytes(far.at[pl.ds(2 * t, 2)], scatter_recv.at[t, 0])
        for b, u, v, first, second in routes(t):
            up, down = (u + 1) % RING, (u + 3) % RING
            partial[b, up, 0:2] += far[b, 0]
            scatter_send_to(t, 2, partial.at[b, up], near.at[b, 0], first(1))
            partial[b, down, 2:4] += far[b, 1]
            scatter_send_to(t, 3, partial.at[b, down], near.at[b, 1], first(3))

    def scatter_third(t):
        await_bytes(near.at[pl.ds(2 * t, 2)], scatter_recv.at[t, 1])
        for b, u, v, first, second in routes(t):
            partial[b, u] += near[b, 0] + near[b, 1]

    def scatter_turn(t):
        for b, u, v, first, second in routes(t):
            block = partial.at[b, u, (v + 2) % RING]
            scatter_send_to(t, 4, block.at[pl.ds(0, HALF)], far_tile.at[b, 0], second(1))
            scatter_send_to(t, 5, block.at[pl.ds(HALF, HALF)], far_tile.at[b, 1], second(3))

    def scatter_fourth(t):
        await_bytes(far_tile.at[pl.ds(2 * t, 2)], scatter_recv.at[t, 2])
        for b, u, v, first, second in routes(t):
            up, down = (v + 1) % RING, (v + 3) % RING
            partial[b, u, up, 0:HALF] += far_tile[b, 0]
            scatter_send_to(t, 6, partial.at[b, u, up], near_tile.at[b, 0], second(1))
            partial[b, u, down, HALF:W] += far_tile[b, 1]
            scatter_send_to(t, 7, partial.at[b, u, down], near_tile.at[b, 1], second(3))

    def finish(t):
        await_bytes(near_tile.at[pl.ds(2 * t, 2)], scatter_recv.at[t, 3])
        for h, (b, u, v, first, second) in enumerate(routes(t)):
            product = partial[b, u, v] + near_tile[b, 0] + near_tile[b, 1]
            panel[t, :, h * W:(h + 1) * W] = -(product * mask[pl.ds(b, 1), :])
        columns = aligned(t * COLS, COLS)
        pltpu.make_async_copy(panel.at[t], panel_hbm.at[:, columns], out_sem.at[0]).start()

    def correct(t):
        for h in range(2):
            correction[t, h * W:(h + 1) * W] = lax.dot_general(
                gathered[t, prow, :, h * W:(h + 1) * W], panel[t, :, h * W:(h + 1) * W],
                (((0,), (0,)), ((), ())),
                precision=lax.Precision.HIGHEST, preferred_element_type=F32,
            )

    def ring_send(start, end):
        for t in range(start, end):
            for h, (step, slot) in enumerate(((along_y, y), (along_x, x))):
                source = gathered.at[t, prow, :, pl.ds(h * W, W)]
                ring_lower[t - EARLY, h, slot] = source[...]
                for k in range(1, RING):
                    send(source, ring_lower.at[t - EARLY, h, slot], ring_sem.at[0], ring_sem.at[1], step(k))

    def correct_early(t):
        for h, (b, u, v, first, second) in enumerate(routes(t)):
            for k in range(RING):
                ring_panel[k] = -(partial[b, u, k] * ring_mask[h, k, pl.ds(b, 1), :])
            correction[t, h * W:(h + 1) * W] = lax.dot_general(
                ring_lower[t - EARLY, h].reshape(RING * W, W), ring_panel[...].reshape(RING * W, W),
                (((0,), (0,)), ((), ())),
                precision=lax.Precision.HIGHEST, preferred_element_type=F32,
            )

    def reduce_send_to(t, stage, source, target, device, sender=None):
        send(source, target, reduce_send.at[stage if sender is None else sender], reduce_recv.at[t, stage], device)

    def axes(t):
        even = t % 2 == 0
        x_devices, y_devices = [along_x(k)[1] for k in range(RING)], [along_y(k)[1] for k in range(RING)]
        u_devices = [(prow, jnp.where(even, a, b)) for a, b in zip(x_devices, y_devices)]
        v_devices = [(prow, jnp.where(even, b, a)) for a, b in zip(x_devices, y_devices)]
        return jnp.where(even, x, y), jnp.where(even, y, x), u_devices, v_devices

    def reduce_first(t):
        for k in range(1, NP):
            rows = aligned(((prow + k) % NP) * 32, 32)
            reduce_send_to(t, 0, correction.at[t, rows], prow_in.at[k, t], along_prow(k))

    def sum_prow(t):
        await_bytes(prow_in.at[pl.ds(1, NP - 1), t], reduce_recv.at[t, 0])
        total = correction[t, own_rows]
        for k in range(1, NP):
            total += prow_in[k, t]
        return total

    def spread_prow(t):
        for k in range(1, NP):
            ref = diag.at[t, own_rows]
            reduce_send_to(t, 4, ref, ref, along_prow(k))

    few = pl.ds(0, 8)

    def reduce_second(t):
        u, v, u_devices, v_devices = axes(t)
        x_in[0, t] = sum_prow(t)
        for k in range(1, RING):
            rows = aligned(((u + k) % RING) * 8, 8)
            reduce_send_to(t, 1, x_in.at[0, t, rows], x_in.at[k, t, few], u_devices[k])

    def reduce_third(t):
        u, v, u_devices, v_devices = axes(t)
        await_bytes(x_in.at[pl.ds(1, RING - 1), t, few], reduce_recv.at[t, 1])
        total = x_in[0, t, aligned(u * 8, 8)]
        for k in range(1, RING):
            total += x_in[k, t, few]
        y_in[v, t, few] = total
        for k in range(1, RING):
            ref = y_in.at[v, t, few]
            reduce_send_to(t, 2, ref, ref, v_devices[k])

    def reduce_fourth(t):
        u, v, u_devices, v_devices = axes(t)
        await_bytes(y_in.at[pl.ds(0, RING - 1), t, few], reduce_recv.at[t, 2])
        total = (y_in[0, t, few] + y_in[1, t, few]) + (y_in[2, t, few] + y_in[3, t, few])
        rows = aligned(prow * 32 + u * 8, 8)
        diag[t, rows] = pivot[t, aligned(u * 8, 8)] - total
        for k in range(1, RING):
            ref = diag.at[t, rows]
            reduce_send_to(t, 3, ref, ref, u_devices[k])

    def reduce_fifth(t):
        await_bytes(diag.at[t, pl.ds(0, 24)], reduce_recv.at[t, 3])
        spread_prow(t)

    def reduce_last(t):
        await_bytes(diag.at[t, pl.ds(0, 224)], reduce_recv.at[t, 4])
        pltpu.make_async_copy(diag.at[t], diag_hbm.at[t], out_sem.at[1]).start()

    def last_second():
        x_in[x, LAST] = sum_prow(LAST)
        for k in range(1, RING):
            ref = x_in.at[x, LAST]
            reduce_send_to(LAST, 1, ref, ref, along_x(k), 5)

    def last_third():
        await_bytes(x_in.at[pl.ds(0, RING - 1), LAST], reduce_recv.at[LAST, 1])
        y_in[y, LAST] = (x_in[0, LAST] + x_in[1, LAST]) + (x_in[2, LAST] + x_in[3, LAST])
        for k in range(1, RING):
            ref = y_in.at[y, LAST]
            reduce_send_to(LAST, 2, ref, ref, along_y(k), 6)

    def last_fourth():
        await_bytes(y_in.at[pl.ds(0, RING - 1), LAST], reduce_recv.at[LAST, 2])
        total = (y_in[0, LAST] + y_in[1, LAST]) + (y_in[2, LAST] + y_in[3, LAST])
        diag[LAST, own_rows] = pivot[LAST] - total
        spread_prow(LAST)

    def prepare():
        await_bytes(gathered.at[pl.ds(1, PAIRS - 1), prow], lower_sem.at[1])
        ring_send(EARLY, 6)

        @pl.loop(0, 128)
        def _(i):
            part = i // 32

            @pl.when(i % 32 == 0)
            def _():
                await_bytes(partial.at[pl.ds(2 * part, 2)], a_sem.at[part])

            rows = aligned(i * 16, 16)
            for r in range(NP):
                high, low = split(partial[i // 16, (i // 4) % 4, i % 4, pl.ds(r, 16, stride=8), :])
                a_high[rows, r * W:(r + 1) * W] = high
                a_low[rows, r * W:(r + 1) * W] = low

        await_bytes(pivot, pivot_sem)

    @pl.loop(-2, PAIRS + 7)
    def _(step):
        def at(lag, body, first=0, end=PAIRS):
            t = step - lag

            @pl.when((t >= first) & (t < end))
            def _():
                body(t)

        def once(when, body, *args):
            @pl.when(step == when)
            def _():
                body(*args)

        def late(when, body, first=LATE, end=PAIRS):
            @pl.when(step == when)
            def _():
                @pl.loop(first, end)
                def _(t):
                    body(t)

        at(10, reduce_last, 0, EARLY)
        at(9, reduce_fifth, 0, EARLY)
        at(8, reduce_fourth, 0, EARLY)
        at(7, reduce_third, 0, EARLY)
        at(6, reduce_second, 0, EARLY)
        late(LAST + 6, finish, LATE, MIDDLE)
        at(8, reduce_last, EARLY, LAST)
        at(7, reduce_fifth, EARLY, LAST)
        at(6, reduce_fourth, EARLY, LAST)
        at(5, reduce_third, EARLY, LAST)
        at(4, reduce_second, EARLY, LAST)
        once(LAST + 7, reduce_last, LAST)
        once(LAST + 6, last_fourth)
        once(LAST + 5, last_third)
        once(LAST + 4, last_second)
        late(LAST + 4, scatter_fourth, LATE, MIDDLE)
        late(LAST + 5, scatter_fourth, MIDDLE, PAIRS)
        late(LAST + 6, finish, MIDDLE, PAIRS)
        at(2, scatter_second)
        once(EARLY + 3, await_bytes, ring_lower.at[:, :, pl.ds(0, RING - 1)], ring_sem.at[1])
        late(LAST + 3, scatter_turn, LATE, LAST)
        at(3, scatter_third)
        at(3, scatter_turn, 0, LATE)
        at(3, scatter_turn, LAST)
        at(3, correct_early, EARLY)
        at(3, reduce_first, EARLY)
        at(4, scatter_fourth, 0, LATE)
        at(5, finish, 0, LATE)
        at(5, correct, 0, EARLY)
        at(5, reduce_first, 0, EARLY)
        once(0, multiply_first)
        at(0, gather_third, 1)
        at(0, gather_wait, 1)
        at(0, multiply, 1)
        at(0, multiply_rows(0), 1)
        at(0, multiply_rows(1), 1)
        at(0, scatter_first)
        once(0, ring_send, 6, PAIRS)
        once(-1, prepare)
        at(-1, gather_second)
        at(-2, gather_first)

    for which in range(8):
        ref = gathered.at[:, 0]
        await_bytes(ref.at[:, pl.ds(0, HALF)] if which in (5, 6) else ref, gather_send.at[which])
        buffer = (far, near, far_tile, near_tile)[which // 2]
        await_bytes(buffer.at[:, which % 2], scatter_send.at[which])
    await_bytes(ring_lower.at[:, :, pl.ds(0, RING - 1)], ring_sem.at[0])
    await_bytes(prow_in.at[pl.ds(1, NP - 1)], reduce_send.at[0])
    await_bytes(x_in.at[pl.ds(1, RING - 1), pl.ds(0, LAST), few], reduce_send.at[1])
    await_bytes(y_in.at[pl.ds(0, RING - 1), pl.ds(0, LAST), few], reduce_send.at[2])
    await_bytes(diag.at[pl.ds(0, LAST), pl.ds(0, 24)], reduce_send.at[3])
    await_bytes(diag.at[:, pl.ds(0, 224)], reduce_send.at[4])
    await_bytes(x_in.at[pl.ds(0, RING - 1), LAST], reduce_send.at[5])
    await_bytes(y_in.at[pl.ds(0, RING - 1), LAST], reduce_send.at[6])
    await_bytes(panel, out_sem.at[0])
    await_bytes(diag, out_sem.at[1])


def hand_over(panel_in, diag_in, panel_out, diag_out, panel_space, diag_space, sem):
    def parts(panel, diag):
        for k in range(4):
            yield panel.at[pl.ds(k * W // 4, W // 4)]
            yield diag.at[pl.ds(k * 2, 2)]

    stages = [list(parts(*refs)) for refs in (
        (panel_in, diag_in), (panel_space, diag_space), (panel_out, diag_out))]
    loads, stores = (
        [pltpu.make_async_copy(a, b, sem.at[n, k]) for k, (a, b) in enumerate(zip(*stages[n:n + 2]))]
        for n in range(2)
    )
    for load in loads:
        load.start()
    for load, store in zip(loads, stores):
        load.wait()
        store.start()
    for store in stores:
        store.wait()


def on_device(ancestor_inverse, lower_panel, structure, pivot_inverse):
    rows = ancestor_inverse.shape[0]
    blocks = ancestor_inverse.reshape(8, 4, 4, W, W)
    pivot_pairs = pivot_inverse.reshape(PAIRS, COLS, W)
    vmem = pl.BlockSpec(memory_space=pltpu.VMEM)
    hbm = pl.BlockSpec(memory_space=pl.ANY)
    depth = NP * W
    dma = pltpu.SemaphoreType.DMA
    out_shape = (
        jax.ShapeDtypeStruct(lower_panel.shape, F32),
        jax.ShapeDtypeStruct(pivot_pairs.shape, F32),
    )
    panel, diag = pl.pallas_call(
        kernel,
        out_shape=out_shape,
        in_specs=[hbm, hbm, vmem, hbm],
        out_specs=(hbm, hbm),
        scratch_shapes=[
            pltpu.VMEM((rows, depth), BF16),
            pltpu.VMEM((rows, depth), BF16),
            pltpu.VMEM((depth, COLS), BF16),
            pltpu.VMEM((depth, COLS), BF16),
            pltpu.VMEM((16, W), F32),
            pltpu.VMEM((2, RING, 16, W), F32),
            pltpu.VMEM((PAIRS, NP, W, COLS), F32),
            pltpu.VMEM((16, RING, RING, W, W), F32),
            pltpu.VMEM((16, 2, 2, W, W), F32),
            pltpu.VMEM((16, 2, 4, W, W), F32),
            pltpu.VMEM((16, 2, HALF, W), F32),
            pltpu.VMEM((16, 2, W, W), F32),
            pltpu.VMEM((PAIRS, W, COLS), F32),
            pltpu.VMEM((PAIRS, COLS, W), F32),
            pltpu.VMEM((PAIRS - EARLY, 2, RING, W, W), F32),
            pltpu.VMEM((RING, W, W), F32),
            pltpu.VMEM((NP, PAIRS, 32, W), F32),
            pltpu.VMEM((RING, PAIRS, 32, W), F32),
            pltpu.VMEM((RING, PAIRS, 32, W), F32),
            pltpu.VMEM((PAIRS, 32, W), F32),
            pltpu.VMEM((PAIRS, COLS, W), F32),
            dma((4,)),
            dma((2,)),
            dma,
            dma((2,)),
            dma((8,)),
            dma((PAIRS, 7)),
            dma((8,)),
            dma((PAIRS, 4)),
            dma((7,)),
            dma((PAIRS, 5)),
            dma((2,)),
        ],
        compiler_params=pltpu.CompilerParams(
            collective_id=0, has_side_effects=True, vmem_limit_bytes=62 * 1024 * 1024,
        ),
        cost_estimate=pl.CostEstimate(
            flops=2 * 3 * rows * depth * lower_panel.shape[1], bytes_accessed=12 << 20, transcendentals=0,
        ),
    )(blocks, lower_panel, structure, pivot_pairs)
    panel, diag = pl.pallas_call(
        hand_over,
        out_shape=out_shape,
        in_specs=[hbm, hbm],
        out_specs=(hbm, hbm),
        scratch_shapes=[
            pltpu.VMEM(out_shape[0].shape, F32), pltpu.VMEM(out_shape[1].shape, F32), dma((2, 8)),
        ],
        compiler_params=pltpu.CompilerParams(vmem_limit_bytes=62 * 1024 * 1024),
    )(panel, diag)
    return panel, diag.reshape(pivot_inverse.shape)


def solution(mesh):
    return jax.shard_map(
        on_device,
        mesh=mesh,
        in_specs=(P("prow", None, "pcol", None), P(("prow", "pcol"), None), P(), P()),
        out_specs=(P(("prow", "pcol"), None), P()),
        check_vma=False,
    )
```

```python
import jax
import jax.numpy as jnp
from jax import lax
from jax.experimental import pallas as pl
from jax.experimental.pallas import tpu as pltpu
from jax.sharding import PartitionSpec as P

F32 = jnp.float32
BF16 = jnp.bfloat16
MESH = pl.DeviceIdType.MESH
W = 128
HALF = W // 2
NP = 8
RING = 4
PAIRS = 8
LAST = PAIRS - 1
COLS = 2 * W
EARLY = 2
LATE = 2
MIDDLE = 4


def split(value):
    high = value.astype(BF16)
    low = (value - high.astype(F32)).astype(BF16)
    return high, low


def product(left, right):
    contract = (((0,), (0,)), ((), ()))
    (left_high, left_low), (right_high, right_low) = split(left), split(right)
    total = lax.dot_general(left_high, right_high, contract, preferred_element_type=F32)
    total += lax.dot_general(left_low, right_high, contract, preferred_element_type=F32)
    total += lax.dot_general(left_high, right_low, contract, preferred_element_type=F32)
    return total


def aligned(start, size):
    return pl.ds(pl.multiple_of(start, size), size)


def kernel(
    a_hbm, lower_hbm, structure_ref, pivot_hbm, panel_hbm, diag_hbm,
    a_high, a_low, b_high, b_low, mask, ring_mask, gathered, partial,
    far, near, far_tile, near_tile, panel, correction, ring_lower, ring_panel,
    prow_in, x_in, y_in, pivot, diag,
    a_sem, lower_sem, pivot_sem, out_sem, gather_send, gather_recv,
    scatter_send, scatter_recv, reduce_send, reduce_recv, ring_sem,
):
    prow, pcol = lax.axis_index("prow"), lax.axis_index("pcol")
    z, core = prow // 2, prow % 2
    x, y = pcol // RING, pcol % RING

    def along_x(step):
        return (prow, ((x + step) % RING) * RING + y)

    def along_y(step):
        return (prow, x * RING + (y + step) % RING)

    def along_prow(step):
        return ((prow + step) % NP, pcol)

    def tile_of(step, which):
        return ((z + step) % RING) * 2 + which

    sibling = (tile_of(0, 1 - core), pcol)
    z_next = (tile_of(1, core), pcol)
    z_last = (tile_of(3, core), pcol)

    def send(source, target, send_sem, recv_sem, device):
        pltpu.make_async_remote_copy(
            src_ref=source, dst_ref=target, send_sem=send_sem, recv_sem=recv_sem,
            device_id=device, device_id_type=MESH,
        ).start()

    def await_bytes(ref, sem):
        pltpu.make_async_copy(ref, ref, sem).wait()

    barrier = pltpu.get_barrier_semaphore()
    partners = [along_prow(k) for k in range(1, NP)]
    partners += [along_x(k) for k in range(1, RING)]
    partners += [along_y(k) for k in range(1, RING)]
    for device in partners:
        pl.semaphore_signal(barrier, inc=1, device_id=device, device_id_type=MESH)

    for t in range(PAIRS):
        pltpu.make_async_copy(
            lower_hbm.at[:, pl.ds(t * COLS, COLS)], gathered.at[t, prow], lower_sem.at[min(t, 1)]
        ).start()
    for part in range(4):
        pltpu.make_async_copy(
            a_hbm.at[pl.ds(2 * part, 2)], partial.at[pl.ds(2 * part, 2)], a_sem.at[part]
        ).start()
    own_rows = aligned(prow * 32, 32)
    pltpu.make_async_copy(pivot_hbm.at[:, own_rows], pivot, pivot_sem).start()

    def member(tile):
        listed = jnp.where(structure_ref[...] == prow * 16 + tile, 1.0, 0.0).astype(F32)
        return jnp.broadcast_to(jnp.max(listed, axis=1, keepdims=True), mask.shape)

    mask[...] = member(pcol)
    for k in range(RING):
        ring_mask[0, k] = member(x * RING + k)
        ring_mask[1, k] = member(k * RING + y)

    await_bytes(gathered.at[0, prow], lower_sem.at[0])
    pl.semaphore_wait(barrier, len(partners))
    await_bytes(gathered.at[pl.ds(1, PAIRS - 1), prow], lower_sem.at[1])

    def gather_send_to(t, ref, which, recv, device):
        send(ref, ref, gather_send.at[which], recv, device)

    def gather_first(t):
        ref = gathered.at[t, prow]
        gather_send_to(t, ref, 0, gather_recv.at[t, 0], z_next)
        gather_send_to(t, ref, 1, gather_recv.at[t, 1], z_last)
        gather_send_to(t, ref, 2, gather_recv.at[t, 3], sibling)

    def gather_second(t):
        ref = gathered.at[t, tile_of(3, core)]
        await_bytes(ref, gather_recv.at[t, 0])
        gather_send_to(t, ref.at[pl.ds(0, HALF)], 5, gather_recv.at[t, 2], z_next)
        gather_send_to(t, ref, 3, gather_recv.at[t, 4], sibling)
        ref = gathered.at[t, tile_of(1, core)]
        await_bytes(ref, gather_recv.at[t, 1])
        gather_send_to(t, ref.at[pl.ds(HALF, HALF)], 6, gather_recv.at[t, 2], z_last)
        gather_send_to(t, ref, 4, gather_recv.at[t, 5], sibling)

    def gather_third(t):
        ref = gathered.at[t, tile_of(2, core)]
        await_bytes(ref, gather_recv.at[t, 2])
        gather_send_to(t, ref, 7, gather_recv.at[t, 6], sibling)

    def gather_wait(t):
        for k, step in enumerate((0, 3, 1, 2)):
            await_bytes(gathered.at[t, tile_of(step, 1 - core)], gather_recv.at[t, 3 + k])

    def multiply(t):
        for tile in range(NP):
            high, low = split(gathered[t, tile])
            b_high[tile * W:(tile + 1) * W] = high
            b_low[tile * W:(tile + 1) * W] = low

    def multiply_rows(h):
        def body(t):
            rows = pl.ds(h * 8 * W, 8 * W)
            total = jnp.dot(a_high[rows], b_high[...], preferred_element_type=F32)
            total += jnp.dot(a_low[rows], b_high[...], preferred_element_type=F32)
            total += jnp.dot(a_high[rows], b_low[...], preferred_element_type=F32)
            for n in range(8):
                i, j = h * 2 + n // 4, n % 4
                block = total[n * W:(n + 1) * W]
                partial[2 * t, i, j] = block[:, :W]
                partial[2 * t + 1, j, i] = block[:, W:]
        return body

    def multiply_first():
        @pl.loop(0, RING)
        def _(k):
            step = jnp.where(k == 0, 0, jnp.where(k == 1, 3, jnp.where(k == 2, 1, 2)))

            @pl.when(k == 3)
            def _():
                gather_second(1)
                gather_first(2)
                gather_third(0)

            chip = (z + step) % RING
            depth = aligned(chip * COLS, COLS)
            await_bytes(gathered.at[0, chip * 2 + 1 - core], gather_recv.at[0, 3 + k])
            for which in range(2):
                high, low = split(gathered[0, chip * 2 + which])
                b_high[which * W:(which + 1) * W] = high
                b_low[which * W:(which + 1) * W] = low

            high, low = b_high[0:COLS], b_low[0:COLS]

            @pl.loop(0, 2)
            def _(h):
                rows = aligned(h * 8 * W, 8 * W)
                total = jnp.dot(a_high[rows, depth], high, preferred_element_type=F32)
                total += jnp.dot(a_low[rows, depth], high, preferred_element_type=F32)
                total += jnp.dot(a_high[rows, depth], low, preferred_element_type=F32)
                for n in range(8):
                    i, j = h * 2 + n // 4, n % 4
                    block = total[n * W:(n + 1) * W]
                    partial[0, i, j] = block[:, :W] + jnp.where(k == 0, 0.0, partial[0, i, j])
                    partial[1, j, i] = block[:, W:] + jnp.where(k == 0, 0.0, partial[1, j, i])

    def routes(t):
        return (
            (2 * t, x, y, along_x, along_y),
            (2 * t + 1, y, x, along_y, along_x),
        )

    def scatter_send_to(t, which, source, target, device):
        send(source, target, scatter_send.at[which], scatter_recv.at[t, which // 2], device)

    def scatter_first(t):
        for b, u, v, first, second in routes(t):
            block = partial.at[b, (u + 2) % RING]
            scatter_send_to(t, 0, block.at[pl.ds(0, 2)], far.at[b, 0], first(1))
            scatter_send_to(t, 1, block.at[pl.ds(2, 2)], far.at[b, 1], first(3))

    def scatter_second(t):
        await_bytes(far.at[pl.ds(2 * t, 2)], scatter_recv.at[t, 0])
        for b, u, v, first, second in routes(t):
            up, down = (u + 1) % RING, (u + 3) % RING
            partial[b, up, 0:2] += far[b, 0]
            scatter_send_to(t, 2, partial.at[b, up], near.at[b, 0], first(1))
            partial[b, down, 2:4] += far[b, 1]
            scatter_send_to(t, 3, partial.at[b, down], near.at[b, 1], first(3))

    def scatter_third(t):
        await_bytes(near.at[pl.ds(2 * t, 2)], scatter_recv.at[t, 1])
        for b, u, v, first, second in routes(t):
            partial[b, u] += near[b, 0] + near[b, 1]

    def scatter_turn(t):
        for b, u, v, first, second in routes(t):
            block = partial.at[b, u, (v + 2) % RING]
            scatter_send_to(t, 4, block.at[pl.ds(0, HALF)], far_tile.at[b, 0], second(1))
            scatter_send_to(t, 5, block.at[pl.ds(HALF, HALF)], far_tile.at[b, 1], second(3))

    def scatter_fourth(t):
        await_bytes(far_tile.at[pl.ds(2 * t, 2)], scatter_recv.at[t, 2])
        for b, u, v, first, second in routes(t):
            up, down = (v + 1) % RING, (v + 3) % RING
            partial[b, u, up, 0:HALF] += far_tile[b, 0]
            scatter_send_to(t, 6, partial.at[b, u, up], near_tile.at[b, 0], second(1))
            partial[b, u, down, HALF:W] += far_tile[b, 1]
            scatter_send_to(t, 7, partial.at[b, u, down], near_tile.at[b, 1], second(3))

    def finish(t):
        await_bytes(near_tile.at[pl.ds(2 * t, 2)], scatter_recv.at[t, 3])
        for h, (b, u, v, first, second) in enumerate(routes(t)):
            total = partial[b, u, v] + near_tile[b, 0] + near_tile[b, 1]
            panel[t, :, h * W:(h + 1) * W] = -(total * mask[pl.ds(b, 1), :])
        columns = aligned(t * COLS, COLS)
        pltpu.make_async_copy(panel.at[t], panel_hbm.at[:, columns], out_sem.at[0]).start()

    def correct(t):
        for h in range(2):
            correction[t, h * W:(h + 1) * W] = lax.dot_general(
                gathered[t, prow, :, h * W:(h + 1) * W], panel[t, :, h * W:(h + 1) * W],
                (((0,), (0,)), ((), ())),
                precision=lax.Precision.HIGHEST, preferred_element_type=F32,
            )

    def ring_send():
        for t in range(EARLY, PAIRS):
            for h, (step, slot) in enumerate(((along_y, y), (along_x, x))):
                source = gathered.at[t, prow, :, pl.ds(h * W, W)]
                ring_lower[t - EARLY, h, slot] = source[...]
                for k in range(1, RING):
                    send(source, ring_lower.at[t - EARLY, h, slot], ring_sem.at[0], ring_sem.at[1], step(k))

    def correct_early(t):
        for h, (b, u, v, first, second) in enumerate(routes(t)):
            for k in range(RING):
                ring_panel[k] = -(partial[b, u, k] * ring_mask[h, k, pl.ds(b, 1), :])
            correction[t, h * W:(h + 1) * W] = product(
                ring_lower[t - EARLY, h].reshape(RING * W, W), ring_panel[...].reshape(RING * W, W)
            )

    def reduce_send_to(t, stage, source, target, device, sender=None):
        send(source, target, reduce_send.at[stage if sender is None else sender], reduce_recv.at[t, stage], device)

    def axes(t):
        even = t % 2 == 0
        x_devices, y_devices = [along_x(k)[1] for k in range(RING)], [along_y(k)[1] for k in range(RING)]
        u_devices = [(prow, jnp.where(even, a, b)) for a, b in zip(x_devices, y_devices)]
        v_devices = [(prow, jnp.where(even, b, a)) for a, b in zip(x_devices, y_devices)]
        return jnp.where(even, x, y), jnp.where(even, y, x), u_devices, v_devices

    def reduce_first(t):
        for k in range(1, NP):
            rows = aligned(((prow + k) % NP) * 32, 32)
            reduce_send_to(t, 0, correction.at[t, rows], prow_in.at[k, t], along_prow(k))

    def sum_prow(t):
        await_bytes(prow_in.at[pl.ds(1, NP - 1), t], reduce_recv.at[t, 0])
        total = correction[t, own_rows]
        for k in range(1, NP):
            total += prow_in[k, t]
        return total

    def spread_prow(t):
        for k in range(1, NP):
            ref = diag.at[t, own_rows]
            reduce_send_to(t, 4, ref, ref, along_prow(k))

    few = pl.ds(0, 8)

    def reduce_second(t):
        u, v, u_devices, v_devices = axes(t)
        x_in[0, t] = sum_prow(t)
        for k in range(1, RING):
            rows = aligned(((u + k) % RING) * 8, 8)
            reduce_send_to(t, 1, x_in.at[0, t, rows], x_in.at[k, t, few], u_devices[k])

    def reduce_third(t):
        u, v, u_devices, v_devices = axes(t)
        await_bytes(x_in.at[pl.ds(1, RING - 1), t, few], reduce_recv.at[t, 1])
        total = x_in[0, t, aligned(u * 8, 8)]
        for k in range(1, RING):
            total += x_in[k, t, few]
        y_in[v, t, few] = total
        for k in range(1, RING):
            ref = y_in.at[v, t, few]
            reduce_send_to(t, 2, ref, ref, v_devices[k])

    def reduce_fourth(t):
        u, v, u_devices, v_devices = axes(t)
        await_bytes(y_in.at[pl.ds(0, RING - 1), t, few], reduce_recv.at[t, 2])
        total = (y_in[0, t, few] + y_in[1, t, few]) + (y_in[2, t, few] + y_in[3, t, few])
        rows = aligned(prow * 32 + u * 8, 8)
        diag[t, rows] = pivot[t, aligned(u * 8, 8)] - total
        for k in range(1, RING):
            ref = diag.at[t, rows]
            reduce_send_to(t, 3, ref, ref, u_devices[k])

    def reduce_fifth(t):
        await_bytes(diag.at[t, pl.ds(0, 24)], reduce_recv.at[t, 3])
        spread_prow(t)

    def reduce_last(t):
        await_bytes(diag.at[t, pl.ds(0, 224)], reduce_recv.at[t, 4])
        pltpu.make_async_copy(diag.at[t], diag_hbm.at[t], out_sem.at[1]).start()

    def last_second():
        x_in[x, LAST] = sum_prow(LAST)
        for k in range(1, RING):
            ref = x_in.at[x, LAST]
            reduce_send_to(LAST, 1, ref, ref, along_x(k), 5)

    def last_third():
        await_bytes(x_in.at[pl.ds(0, RING - 1), LAST], reduce_recv.at[LAST, 1])
        y_in[y, LAST] = (x_in[0, LAST] + x_in[1, LAST]) + (x_in[2, LAST] + x_in[3, LAST])
        for k in range(1, RING):
            ref = y_in.at[y, LAST]
            reduce_send_to(LAST, 2, ref, ref, along_y(k), 6)

    def last_fourth():
        await_bytes(y_in.at[pl.ds(0, RING - 1), LAST], reduce_recv.at[LAST, 2])
        total = (y_in[0, LAST] + y_in[1, LAST]) + (y_in[2, LAST] + y_in[3, LAST])
        diag[LAST, own_rows] = pivot[LAST] - total
        spread_prow(LAST)

    def prepare():
        ring_send()

        @pl.loop(0, 128)
        def _(i):
            part = i // 32

            @pl.when(i % 32 == 0)
            def _():
                await_bytes(partial.at[pl.ds(2 * part, 2)], a_sem.at[part])

            rows = aligned(i * 16, 16)
            for r in range(NP):
                high, low = split(partial[i // 16, (i // 4) % 4, i % 4, pl.ds(r, 16, stride=8), :])
                a_high[rows, r * W:(r + 1) * W] = high
                a_low[rows, r * W:(r + 1) * W] = low

        await_bytes(pivot, pivot_sem)

    @pl.loop(-2, PAIRS + 7)
    def _(step):
        def at(lag, body, first=0, end=PAIRS):
            t = step - lag

            @pl.when((t >= first) & (t < end))
            def _():
                body(t)

        def once(when, body, *args):
            @pl.when(step == when)
            def _():
                body(*args)

        def late(when, body, first=LATE, end=PAIRS):
            @pl.when(step == when)
            def _():
                @pl.loop(first, end)
                def _(t):
                    body(t)

        at(0, gather_third, 1)
        at(10, reduce_last, 0, EARLY)
        at(9, reduce_fifth, 0, EARLY)
        at(8, reduce_fourth, 0, EARLY)
        at(7, reduce_third, 0, EARLY)
        at(6, reduce_second, 0, EARLY)
        late(LAST + 6, finish, LATE, MIDDLE)
        at(8, reduce_last, EARLY, LAST)
        at(7, reduce_fifth, EARLY, LAST)
        at(6, reduce_fourth, EARLY, LAST)
        at(5, reduce_third, EARLY, LAST)
        at(4, reduce_second, EARLY, LAST)
        once(LAST + 7, reduce_last, LAST)
        once(LAST + 6, last_fourth)
        once(LAST + 5, last_third)
        once(LAST + 4, last_second)
        late(LAST + 4, scatter_fourth, LATE, MIDDLE)
        late(LAST + 5, scatter_fourth, MIDDLE, PAIRS)
        late(LAST + 6, finish, MIDDLE, PAIRS)
        at(2, scatter_second)
        once(EARLY + 3, await_bytes, ring_lower.at[:, :, pl.ds(0, RING - 1)], ring_sem.at[1])
        late(LAST + 3, scatter_turn, LATE, LAST)
        at(3, scatter_third)
        at(3, scatter_turn, 0, LATE)
        at(3, scatter_turn, LAST)
        at(3, correct_early, EARLY)
        at(3, reduce_first, EARLY)
        at(4, scatter_fourth, 0, LATE)
        at(5, finish, 0, LATE)
        at(5, correct, 0, EARLY)
        at(5, reduce_first, 0, EARLY)
        once(0, multiply_first)
        at(0, gather_wait, 1)
        at(0, multiply, 1)
        at(0, multiply_rows(0), 1)
        at(-1, gather_second, 2)
        at(-2, gather_first, 3)
        at(0, multiply_rows(1), 1)
        at(0, scatter_first)
        at(-2, gather_first, 0, 2)
        once(-1, prepare)
        at(-1, gather_second, 0, 1)

    for which in range(8):
        ref = gathered.at[:, 0]
        await_bytes(ref.at[:, pl.ds(0, HALF)] if which in (5, 6) else ref, gather_send.at[which])
        buffer = (far, near, far_tile, near_tile)[which // 2]
        await_bytes(buffer.at[:, which % 2], scatter_send.at[which])
    await_bytes(ring_lower.at[:, :, pl.ds(0, RING - 1)], ring_sem.at[0])
    await_bytes(prow_in.at[pl.ds(1, NP - 1)], reduce_send.at[0])
    await_bytes(x_in.at[pl.ds(1, RING - 1), pl.ds(0, LAST), few], reduce_send.at[1])
    await_bytes(y_in.at[pl.ds(0, RING - 1), pl.ds(0, LAST), few], reduce_send.at[2])
    await_bytes(diag.at[pl.ds(0, LAST), pl.ds(0, 24)], reduce_send.at[3])
    await_bytes(diag.at[:, pl.ds(0, 224)], reduce_send.at[4])
    await_bytes(x_in.at[pl.ds(0, RING - 1), LAST], reduce_send.at[5])
    await_bytes(y_in.at[pl.ds(0, RING - 1), LAST], reduce_send.at[6])
    await_bytes(panel, out_sem.at[0])
    await_bytes(diag, out_sem.at[1])


def hand_over(panel_in, diag_in, panel_out, diag_out, panel_space, diag_space, sem):
    def parts(panel, diag):
        for k in range(4):
            yield panel.at[pl.ds(k * W // 4, W // 4)]
            yield diag.at[pl.ds(k * 2, 2)]

    stages = [list(parts(*refs)) for refs in (
        (panel_in, diag_in), (panel_space, diag_space), (panel_out, diag_out))]
    loads, stores = (
        [pltpu.make_async_copy(a, b, sem.at[n, k]) for k, (a, b) in enumerate(zip(*stages[n:n + 2]))]
        for n in range(2)
    )
    for load in loads:
        load.start()
    for load, store in zip(loads, stores):
        load.wait()
        store.start()
    for store in stores:
        store.wait()


def on_device(ancestor_inverse, lower_panel, structure, pivot_inverse):
    rows = ancestor_inverse.shape[0]
    blocks = ancestor_inverse.reshape(8, 4, 4, W, W)
    pivot_pairs = pivot_inverse.reshape(PAIRS, COLS, W)
    vmem = pl.BlockSpec(memory_space=pltpu.VMEM)
    hbm = pl.BlockSpec(memory_space=pl.ANY)
    depth = NP * W
    dma = pltpu.SemaphoreType.DMA
    out_shape = (
        jax.ShapeDtypeStruct(lower_panel.shape, F32),
        jax.ShapeDtypeStruct(pivot_pairs.shape, F32),
    )
    panel, diag = pl.pallas_call(
        kernel,
        out_shape=out_shape,
        in_specs=[hbm, hbm, vmem, hbm],
        out_specs=(hbm, hbm),
        scratch_shapes=[
            pltpu.VMEM((rows, depth), BF16),
            pltpu.VMEM((rows, depth), BF16),
            pltpu.VMEM((depth, COLS), BF16),
            pltpu.VMEM((depth, COLS), BF16),
            pltpu.VMEM((16, W), F32),
            pltpu.VMEM((2, RING, 16, W), F32),
            pltpu.VMEM((PAIRS, NP, W, COLS), F32),
            pltpu.VMEM((16, RING, RING, W, W), F32),
            pltpu.VMEM((16, 2, 2, W, W), F32),
            pltpu.VMEM((16, 2, 4, W, W), F32),
            pltpu.VMEM((16, 2, HALF, W), F32),
            pltpu.VMEM((16, 2, W, W), F32),
            pltpu.VMEM((PAIRS, W, COLS), F32),
            pltpu.VMEM((PAIRS, COLS, W), F32),
            pltpu.VMEM((PAIRS - EARLY, 2, RING, W, W), F32),
            pltpu.VMEM((RING, W, W), F32),
            pltpu.VMEM((NP, PAIRS, 32, W), F32),
            pltpu.VMEM((RING, PAIRS, 32, W), F32),
            pltpu.VMEM((RING, PAIRS, 32, W), F32),
            pltpu.VMEM((PAIRS, 32, W), F32),
            pltpu.VMEM((PAIRS, COLS, W), F32),
            dma((4,)),
            dma((2,)),
            dma,
            dma((2,)),
            dma((8,)),
            dma((PAIRS, 7)),
            dma((8,)),
            dma((PAIRS, 4)),
            dma((7,)),
            dma((PAIRS, 5)),
            dma((2,)),
        ],
        compiler_params=pltpu.CompilerParams(
            collective_id=0, has_side_effects=True, vmem_limit_bytes=62 * 1024 * 1024,
        ),
        cost_estimate=pl.CostEstimate(
            flops=2 * 3 * rows * depth * lower_panel.shape[1], bytes_accessed=12 << 20, transcendentals=0,
        ),
    )(blocks, lower_panel, structure, pivot_pairs)
    panel, diag = pl.pallas_call(
        hand_over,
        out_shape=out_shape,
        in_specs=[hbm, hbm],
        out_specs=(hbm, hbm),
        scratch_shapes=[
            pltpu.VMEM(out_shape[0].shape, F32), pltpu.VMEM(out_shape[1].shape, F32), dma((2, 8)),
        ],
        compiler_params=pltpu.CompilerParams(vmem_limit_bytes=62 * 1024 * 1024),
    )(panel, diag)
    return panel, diag.reshape(pivot_inverse.shape)


def solution(mesh):
    return jax.shard_map(
        on_device,
        mesh=mesh,
        in_specs=(P("prow", None, "pcol", None), P(("prow", "pcol"), None), P(), P()),
        out_specs=(P(("prow", "pcol"), None), P()),
        check_vma=False,
    )
```

```python
import jax
import jax.numpy as jnp
from jax import lax
from jax.experimental import pallas as pl
from jax.experimental.pallas import tpu as pltpu
from jax.sharding import PartitionSpec as P

F32 = jnp.float32
BF16 = jnp.bfloat16
MESH = pl.DeviceIdType.MESH
W = 128
HALF = W // 2
NP = 8
RING = 4
PAIRS = 8
LAST = PAIRS - 1
COLS = 2 * W
EARLY = 2
LATE = 2
MIDDLE = 4


def split(value):
    high = value.astype(BF16)
    low = (value - high.astype(F32)).astype(BF16)
    return high, low


def product(left, right):
    contract = (((0,), (0,)), ((), ()))
    (left_high, left_low), (right_high, right_low) = split(left), split(right)
    total = lax.dot_general(left_high, right_high, contract, preferred_element_type=F32)
    total += lax.dot_general(left_low, right_high, contract, preferred_element_type=F32)
    total += lax.dot_general(left_high, right_low, contract, preferred_element_type=F32)
    return total


def aligned(start, size):
    return pl.ds(pl.multiple_of(start, size), size)


def kernel(
    a_hbm, lower_hbm, structure_ref, pivot_hbm, panel_hbm, diag_hbm,
    a_high, a_low, b_high, b_low, mask, ring_mask, gathered, partial,
    far, near, far_tile, near_tile, panel, correction, ring_lower, ring_panel,
    prow_in, x_in, y_in, pivot, diag,
    a_sem, lower_sem, pivot_sem, out_sem, gather_send, gather_recv,
    scatter_send, scatter_recv, reduce_send, reduce_recv, ring_sem,
):
    prow, pcol = lax.axis_index("prow"), lax.axis_index("pcol")
    z, core = prow // 2, prow % 2
    x, y = pcol // RING, pcol % RING

    def along_x(step):
        return (prow, ((x + step) % RING) * RING + y)

    def along_y(step):
        return (prow, x * RING + (y + step) % RING)

    def along_prow(step):
        return ((prow + step) % NP, pcol)

    def tile_of(step, which):
        return ((z + step) % RING) * 2 + which

    sibling = (tile_of(0, 1 - core), pcol)
    z_next = (tile_of(1, core), pcol)
    z_last = (tile_of(3, core), pcol)

    def send(source, target, send_sem, recv_sem, device):
        pltpu.make_async_remote_copy(
            src_ref=source, dst_ref=target, send_sem=send_sem, recv_sem=recv_sem,
            device_id=device, device_id_type=MESH,
        ).start()

    def await_bytes(ref, sem):
        pltpu.make_async_copy(ref, ref, sem).wait()

    barrier = pltpu.get_barrier_semaphore()
    partners = [along_prow(k) for k in range(1, NP)]
    partners += [along_x(k) for k in range(1, RING)]
    partners += [along_y(k) for k in range(1, RING)]
    for device in partners:
        pl.semaphore_signal(barrier, inc=1, device_id=device, device_id_type=MESH)

    for t in range(PAIRS):
        pltpu.make_async_copy(
            lower_hbm.at[:, pl.ds(t * COLS, COLS)], gathered.at[t, prow], lower_sem.at[min(t, 1)]
        ).start()
    for part in range(4):
        pltpu.make_async_copy(
            a_hbm.at[pl.ds(2 * part, 2)], partial.at[pl.ds(2 * part, 2)], a_sem.at[part]
        ).start()
    own_rows = aligned(prow * 32, 32)
    pltpu.make_async_copy(pivot_hbm.at[:, own_rows], pivot, pivot_sem).start()

    def member(tile):
        listed = jnp.where(structure_ref[...] == prow * 16 + tile, 1.0, 0.0).astype(F32)
        return jnp.broadcast_to(jnp.max(listed, axis=1, keepdims=True), mask.shape)

    mask[...] = member(pcol)
    for k in range(RING):
        ring_mask[0, k] = member(x * RING + k)
        ring_mask[1, k] = member(k * RING + y)

    await_bytes(gathered.at[0, prow], lower_sem.at[0])
    pl.semaphore_wait(barrier, len(partners))
    await_bytes(gathered.at[pl.ds(1, PAIRS - 1), prow], lower_sem.at[1])

    def gather_send_to(t, ref, which, recv, device):
        send(ref, ref, gather_send.at[which], recv, device)

    def gather_first(t):
        ref = gathered.at[t, prow]
        gather_send_to(t, ref, 0, gather_recv.at[t, 0], z_next)
        gather_send_to(t, ref, 1, gather_recv.at[t, 1], z_last)
        gather_send_to(t, ref, 2, gather_recv.at[t, 3], sibling)

    def gather_second(t):
        ref = gathered.at[t, tile_of(3, core)]
        await_bytes(ref, gather_recv.at[t, 0])
        gather_send_to(t, ref.at[pl.ds(0, HALF)], 5, gather_recv.at[t, 2], z_next)
        gather_send_to(t, ref, 3, gather_recv.at[t, 4], sibling)
        ref = gathered.at[t, tile_of(1, core)]
        await_bytes(ref, gather_recv.at[t, 1])
        gather_send_to(t, ref.at[pl.ds(HALF, HALF)], 6, gather_recv.at[t, 2], z_last)
        gather_send_to(t, ref, 4, gather_recv.at[t, 5], sibling)

    def gather_third(t):
        ref = gathered.at[t, tile_of(2, core)]
        await_bytes(ref, gather_recv.at[t, 2])
        gather_send_to(t, ref, 7, gather_recv.at[t, 6], sibling)

    def gather_wait(t):
        for k, step in enumerate((0, 3, 1, 2)):
            await_bytes(gathered.at[t, tile_of(step, 1 - core)], gather_recv.at[t, 3 + k])

    def multiply(t):
        for tile in range(NP):
            high, low = split(gathered[t, tile])
            b_high[tile * W:(tile + 1) * W] = high
            b_low[tile * W:(tile + 1) * W] = low

    def multiply_rows(h):
        def body(t):
            rows = pl.ds(h * 8 * W, 8 * W)
            total = jnp.dot(a_high[rows], b_high[...], preferred_element_type=F32)
            total += jnp.dot(a_low[rows], b_high[...], preferred_element_type=F32)
            total += jnp.dot(a_high[rows], b_low[...], preferred_element_type=F32)
            for n in range(8):
                i, j = h * 2 + n // 4, n % 4
                block = total[n * W:(n + 1) * W]
                partial[2 * t, i, j] = block[:, :W]
                partial[2 * t + 1, j, i] = block[:, W:]
        return body

    def multiply_first():
        @pl.loop(0, RING)
        def _(k):
            step = jnp.where(k == 0, 0, jnp.where(k == 1, 3, jnp.where(k == 2, 1, 2)))

            @pl.when(k == 3)
            def _():
                gather_second(1)
                gather_first(2)
                gather_third(0)

            chip = (z + step) % RING
            depth = aligned(chip * COLS, COLS)
            await_bytes(gathered.at[0, chip * 2 + 1 - core], gather_recv.at[0, 3 + k])
            for which in range(2):
                high, low = split(gathered[0, chip * 2 + which])
                b_high[which * W:(which + 1) * W] = high
                b_low[which * W:(which + 1) * W] = low

            high, low = b_high[0:COLS], b_low[0:COLS]

            @pl.loop(0, 2)
            def _(h):
                rows = aligned(h * 8 * W, 8 * W)
                total = jnp.dot(a_high[rows, depth], high, preferred_element_type=F32)
                total += jnp.dot(a_low[rows, depth], high, preferred_element_type=F32)
                total += jnp.dot(a_high[rows, depth], low, preferred_element_type=F32)
                for n in range(8):
                    i, j = h * 2 + n // 4, n % 4
                    block = total[n * W:(n + 1) * W]
                    partial[0, i, j] = block[:, :W] + jnp.where(k == 0, 0.0, partial[0, i, j])
                    partial[1, j, i] = block[:, W:] + jnp.where(k == 0, 0.0, partial[1, j, i])

    def routes(t):
        return (
            (2 * t, x, y, along_x, along_y),
            (2 * t + 1, y, x, along_y, along_x),
        )

    def scatter_send_to(t, which, source, target, device):
        send(source, target, scatter_send.at[which], scatter_recv.at[t, which // 2], device)

    def scatter_first(t, chosen=(0, 1)):
        for b, u, v, first, second in [routes(t)[h] for h in chosen]:
            block = partial.at[b, (u + 2) % RING]
            scatter_send_to(t, 0, block.at[pl.ds(0, 2)], far.at[b, 0], first(1))
            scatter_send_to(t, 1, block.at[pl.ds(2, 2)], far.at[b, 1], first(3))

    def scatter_even(ready):
        def body(t):
            @pl.when(ready)
            def _():
                scatter_first(t, (0,))
        return body

    def scatter_odd(t):
        scatter_first(t, (1,))

    def scatter_second(t):
        await_bytes(far.at[pl.ds(2 * t, 2)], scatter_recv.at[t, 0])
        for b, u, v, first, second in routes(t):
            up, down = (u + 1) % RING, (u + 3) % RING
            partial[b, up, 0:2] += far[b, 0]
            scatter_send_to(t, 2, partial.at[b, up], near.at[b, 0], first(1))
            partial[b, down, 2:4] += far[b, 1]
            scatter_send_to(t, 3, partial.at[b, down], near.at[b, 1], first(3))

    def scatter_third(t):
        await_bytes(near.at[pl.ds(2 * t, 2)], scatter_recv.at[t, 1])
        for b, u, v, first, second in routes(t):
            partial[b, u] += near[b, 0] + near[b, 1]

    def scatter_turn(t):
        for b, u, v, first, second in routes(t):
            block = partial.at[b, u, (v + 2) % RING]
            scatter_send_to(t, 4, block.at[pl.ds(0, HALF)], far_tile.at[b, 0], second(1))
            scatter_send_to(t, 5, block.at[pl.ds(HALF, HALF)], far_tile.at[b, 1], second(3))

    def scatter_fourth(t):
        await_bytes(far_tile.at[pl.ds(2 * t, 2)], scatter_recv.at[t, 2])
        for b, u, v, first, second in routes(t):
            up, down = (v + 1) % RING, (v + 3) % RING
            partial[b, u, up, 0:HALF] += far_tile[b, 0]
            scatter_send_to(t, 6, partial.at[b, u, up], near_tile.at[b, 0], second(1))
            partial[b, u, down, HALF:W] += far_tile[b, 1]
            scatter_send_to(t, 7, partial.at[b, u, down], near_tile.at[b, 1], second(3))

    def finish(t):
        await_bytes(near_tile.at[pl.ds(2 * t, 2)], scatter_recv.at[t, 3])
        for h, (b, u, v, first, second) in enumerate(routes(t)):
            total = partial[b, u, v] + near_tile[b, 0] + near_tile[b, 1]
            panel[t, :, h * W:(h + 1) * W] = -(total * mask[pl.ds(b, 1), :])
        columns = aligned(t * COLS, COLS)
        pltpu.make_async_copy(panel.at[t], panel_hbm.at[:, columns], out_sem.at[0]).start()

    def correct(t):
        for h in range(2):
            correction[t, h * W:(h + 1) * W] = product(
                gathered[t, prow, :, h * W:(h + 1) * W], panel[t, :, h * W:(h + 1) * W]
            )

    def ring_send():
        for t in range(EARLY, PAIRS):
            for h, (step, slot) in enumerate(((along_y, y), (along_x, x))):
                source = gathered.at[t, prow, :, pl.ds(h * W, W)]
                ring_lower[t - EARLY, h, slot] = source[...]
                for k in range(1, RING):
                    send(source, ring_lower.at[t - EARLY, h, slot], ring_sem.at[0], ring_sem.at[1], step(k))

    def correct_early(t):
        for h, (b, u, v, first, second) in enumerate(routes(t)):
            for k in range(RING):
                ring_panel[k] = -(partial[b, u, k] * ring_mask[h, k, pl.ds(b, 1), :])
            correction[t, h * W:(h + 1) * W] = product(
                ring_lower[t - EARLY, h].reshape(RING * W, W), ring_panel[...].reshape(RING * W, W)
            )

    def reduce_send_to(t, stage, source, target, device, sender=None):
        send(source, target, reduce_send.at[stage if sender is None else sender], reduce_recv.at[t, stage], device)

    def axes(t):
        even = t % 2 == 0
        x_devices, y_devices = [along_x(k)[1] for k in range(RING)], [along_y(k)[1] for k in range(RING)]
        u_devices = [(prow, jnp.where(even, a, b)) for a, b in zip(x_devices, y_devices)]
        v_devices = [(prow, jnp.where(even, b, a)) for a, b in zip(x_devices, y_devices)]
        return jnp.where(even, x, y), jnp.where(even, y, x), u_devices, v_devices

    def reduce_first(t):
        for k in range(1, NP):
            rows = aligned(((prow + k) % NP) * 32, 32)
            reduce_send_to(t, 0, correction.at[t, rows], prow_in.at[k, t], along_prow(k))

    def sum_prow(t):
        await_bytes(prow_in.at[pl.ds(1, NP - 1), t], reduce_recv.at[t, 0])
        total = correction[t, own_rows]
        for k in range(1, NP):
            total += prow_in[k, t]
        return total

    def spread_prow(t):
        for k in range(1, NP):
            ref = diag.at[t, own_rows]
            reduce_send_to(t, 4, ref, ref, along_prow(k))

    few = pl.ds(0, 8)

    def reduce_second(t):
        u, v, u_devices, v_devices = axes(t)
        x_in[0, t] = sum_prow(t)
        for k in range(1, RING):
            rows = aligned(((u + k) % RING) * 8, 8)
            reduce_send_to(t, 1, x_in.at[0, t, rows], x_in.at[k, t, few], u_devices[k])

    def reduce_third(t):
        u, v, u_devices, v_devices = axes(t)
        await_bytes(x_in.at[pl.ds(1, RING - 1), t, few], reduce_recv.at[t, 1])
        total = x_in[0, t, aligned(u * 8, 8)]
        for k in range(1, RING):
            total += x_in[k, t, few]
        y_in[v, t, few] = total
        for k in range(1, RING):
            ref = y_in.at[v, t, few]
            reduce_send_to(t, 2, ref, ref, v_devices[k])

    def reduce_fourth(t):
        u, v, u_devices, v_devices = axes(t)
        await_bytes(y_in.at[pl.ds(0, RING - 1), t, few], reduce_recv.at[t, 2])
        total = (y_in[0, t, few] + y_in[1, t, few]) + (y_in[2, t, few] + y_in[3, t, few])
        rows = aligned(prow * 32 + u * 8, 8)
        diag[t, rows] = pivot[t, aligned(u * 8, 8)] - total
        for k in range(1, RING):
            ref = diag.at[t, rows]
            reduce_send_to(t, 3, ref, ref, u_devices[k])

    def reduce_fifth(t):
        await_bytes(diag.at[t, pl.ds(0, 24)], reduce_recv.at[t, 3])
        spread_prow(t)

    def reduce_last(t):
        await_bytes(diag.at[t, pl.ds(0, 224)], reduce_recv.at[t, 4])
        pltpu.make_async_copy(diag.at[t], diag_hbm.at[t], out_sem.at[1]).start()

    def last_second():
        x_in[x, LAST] = sum_prow(LAST)
        for k in range(1, RING):
            ref = x_in.at[x, LAST]
            reduce_send_to(LAST, 1, ref, ref, along_x(k), 5)

    def last_third():
        await_bytes(x_in.at[pl.ds(0, RING - 1), LAST], reduce_recv.at[LAST, 1])
        y_in[y, LAST] = (x_in[0, LAST] + x_in[1, LAST]) + (x_in[2, LAST] + x_in[3, LAST])
        for k in range(1, RING):
            ref = y_in.at[y, LAST]
            reduce_send_to(LAST, 2, ref, ref, along_y(k), 6)

    def last_fourth():
        await_bytes(y_in.at[pl.ds(0, RING - 1), LAST], reduce_recv.at[LAST, 2])
        total = (y_in[0, LAST] + y_in[1, LAST]) + (y_in[2, LAST] + y_in[3, LAST])
        diag[LAST, own_rows] = pivot[LAST] - total
        spread_prow(LAST)

    def prepare():
        ring_send()

        @pl.loop(0, 128)
        def _(i):
            part = i // 32

            @pl.when(i % 32 == 0)
            def _():
                await_bytes(partial.at[pl.ds(2 * part, 2)], a_sem.at[part])

            rows = aligned(i * 16, 16)
            for r in range(NP):
                high, low = split(partial[i // 16, (i // 4) % 4, i % 4, pl.ds(r, 16, stride=8), :])
                a_high[rows, r * W:(r + 1) * W] = high
                a_low[rows, r * W:(r + 1) * W] = low

        await_bytes(pivot, pivot_sem)

    @pl.loop(-2, PAIRS + 7)
    def _(step):
        def at(lag, body, first=0, end=PAIRS):
            t = step - lag

            @pl.when((t >= first) & (t < end))
            def _():
                body(t)

        def once(when, body, *args):
            @pl.when(step == when)
            def _():
                body(*args)

        def late(when, body, first=LATE, end=PAIRS):
            @pl.when(step == when)
            def _():
                @pl.loop(first, end)
                def _(t):
                    body(t)

        at(0, gather_third, 1)
        at(10, reduce_last, 0, EARLY)
        at(9, reduce_fifth, 0, EARLY)
        at(8, reduce_fourth, 0, EARLY)
        at(7, reduce_third, 0, EARLY)
        at(6, reduce_second, 0, EARLY)
        late(LAST + 6, finish, LATE, MIDDLE)
        at(8, reduce_last, EARLY, LAST)
        at(7, reduce_fifth, EARLY, LAST)
        at(6, reduce_fourth, EARLY, LAST)
        at(5, reduce_third, EARLY, LAST)
        at(4, reduce_second, EARLY, LAST)
        once(LAST + 7, reduce_last, LAST)
        once(LAST + 6, last_fourth)
        once(LAST + 5, last_third)
        once(LAST + 4, last_second)
        late(LAST + 4, scatter_fourth, LATE, MIDDLE)
        late(LAST + 5, scatter_fourth, MIDDLE, PAIRS)
        late(LAST + 6, finish, MIDDLE, PAIRS)
        at(2, scatter_second)
        once(EARLY + 3, await_bytes, ring_lower.at[:, :, pl.ds(0, RING - 1)], ring_sem.at[1])
        late(LAST + 3, scatter_turn, LATE, LAST)
        at(3, scatter_third)
        at(3, scatter_turn, 0, LATE)
        at(3, scatter_turn, LAST)
        at(3, correct_early, EARLY)
        at(3, reduce_first, EARLY)
        at(4, scatter_fourth, 0, LATE)
        at(5, finish, 0, LATE)
        at(5, correct, 0, EARLY)
        at(5, reduce_first, 0, EARLY)
        once(0, multiply_first)
        at(0, gather_wait, 1)
        at(0, multiply, 1)
        at(0, multiply_rows(0), 1)
        at(0, scatter_even(x >= 2), 1)
        at(-1, gather_second, 2)
        at(-2, gather_first, 3)
        at(0, multiply_rows(1), 1)
        at(0, scatter_first, 0, 1)
        at(0, scatter_even(x < 2), 1)
        at(0, scatter_odd, 1)
        at(-2, gather_first, 0, 2)
        once(-1, prepare)
        at(-1, gather_second, 0, 1)

    for which in range(8):
        ref = gathered.at[:, 0]
        await_bytes(ref.at[:, pl.ds(0, HALF)] if which in (5, 6) else ref, gather_send.at[which])
        buffer = (far, near, far_tile, near_tile)[which // 2]
        await_bytes(buffer.at[:, which % 2], scatter_send.at[which])
    await_bytes(ring_lower.at[:, :, pl.ds(0, RING - 1)], ring_sem.at[0])
    await_bytes(prow_in.at[pl.ds(1, NP - 1)], reduce_send.at[0])
    await_bytes(x_in.at[pl.ds(1, RING - 1), pl.ds(0, LAST), few], reduce_send.at[1])
    await_bytes(y_in.at[pl.ds(0, RING - 1), pl.ds(0, LAST), few], reduce_send.at[2])
    await_bytes(diag.at[pl.ds(0, LAST), pl.ds(0, 24)], reduce_send.at[3])
    await_bytes(diag.at[:, pl.ds(0, 224)], reduce_send.at[4])
    await_bytes(x_in.at[pl.ds(0, RING - 1), LAST], reduce_send.at[5])
    await_bytes(y_in.at[pl.ds(0, RING - 1), LAST], reduce_send.at[6])
    await_bytes(panel, out_sem.at[0])
    await_bytes(diag, out_sem.at[1])


def hand_over(panel_in, diag_in, panel_out, diag_out, panel_space, diag_space, sem):
    def parts(panel, diag):
        for k in range(4):
            yield panel.at[pl.ds(k * W // 4, W // 4)]
            yield diag.at[pl.ds(k * 2, 2)]

    stages = [list(parts(*refs)) for refs in (
        (panel_in, diag_in), (panel_space, diag_space), (panel_out, diag_out))]
    loads, stores = (
        [pltpu.make_async_copy(a, b, sem.at[n, k]) for k, (a, b) in enumerate(zip(*stages[n:n + 2]))]
        for n in range(2)
    )
    for load in loads:
        load.start()
    for load, store in zip(loads, stores):
        load.wait()
        store.start()
    for store in stores:
        store.wait()


def on_device(ancestor_inverse, lower_panel, structure, pivot_inverse):
    rows = ancestor_inverse.shape[0]
    blocks = ancestor_inverse.reshape(8, 4, 4, W, W)
    pivot_pairs = pivot_inverse.reshape(PAIRS, COLS, W)
    vmem = pl.BlockSpec(memory_space=pltpu.VMEM)
    hbm = pl.BlockSpec(memory_space=pl.ANY)
    depth = NP * W
    dma = pltpu.SemaphoreType.DMA
    out_shape = (
        jax.ShapeDtypeStruct(lower_panel.shape, F32),
        jax.ShapeDtypeStruct(pivot_pairs.shape, F32),
    )
    panel, diag = pl.pallas_call(
        kernel,
        out_shape=out_shape,
        in_specs=[hbm, hbm, vmem, hbm],
        out_specs=(hbm, hbm),
        scratch_shapes=[
            pltpu.VMEM((rows, depth), BF16),
            pltpu.VMEM((rows, depth), BF16),
            pltpu.VMEM((depth, COLS), BF16),
            pltpu.VMEM((depth, COLS), BF16),
            pltpu.VMEM((16, W), F32),
            pltpu.VMEM((2, RING, 16, W), F32),
            pltpu.VMEM((PAIRS, NP, W, COLS), F32),
            pltpu.VMEM((16, RING, RING, W, W), F32),
            pltpu.VMEM((16, 2, 2, W, W), F32),
            pltpu.VMEM((16, 2, 4, W, W), F32),
            pltpu.VMEM((16, 2, HALF, W), F32),
            pltpu.VMEM((16, 2, W, W), F32),
            pltpu.VMEM((PAIRS, W, COLS), F32),
            pltpu.VMEM((PAIRS, COLS, W), F32),
            pltpu.VMEM((PAIRS - EARLY, 2, RING, W, W), F32),
            pltpu.VMEM((RING, W, W), F32),
            pltpu.VMEM((NP, PAIRS, 32, W), F32),
            pltpu.VMEM((RING, PAIRS, 32, W), F32),
            pltpu.VMEM((RING, PAIRS, 32, W), F32),
            pltpu.VMEM((PAIRS, 32, W), F32),
            pltpu.VMEM((PAIRS, COLS, W), F32),
            dma((4,)),
            dma((2,)),
            dma,
            dma((2,)),
            dma((8,)),
            dma((PAIRS, 7)),
            dma((8,)),
            dma((PAIRS, 4)),
            dma((7,)),
            dma((PAIRS, 5)),
            dma((2,)),
        ],
        compiler_params=pltpu.CompilerParams(
            collective_id=0, has_side_effects=True, vmem_limit_bytes=62 * 1024 * 1024,
        ),
        cost_estimate=pl.CostEstimate(
            flops=2 * 3 * rows * depth * lower_panel.shape[1], bytes_accessed=12 << 20, transcendentals=0,
        ),
    )(blocks, lower_panel, structure, pivot_pairs)
    panel, diag = pl.pallas_call(
        hand_over,
        out_shape=out_shape,
        in_specs=[hbm, hbm],
        out_specs=(hbm, hbm),
        scratch_shapes=[
            pltpu.VMEM(out_shape[0].shape, F32), pltpu.VMEM(out_shape[1].shape, F32), dma((2, 8)),
        ],
        compiler_params=pltpu.CompilerParams(vmem_limit_bytes=62 * 1024 * 1024),
    )(panel, diag)
    return panel, diag.reshape(pivot_inverse.shape)


def solution(mesh):
    return jax.shard_map(
        on_device,
        mesh=mesh,
        in_specs=(P("prow", None, "pcol", None), P(("prow", "pcol"), None), P(), P()),
        out_specs=(P(("prow", "pcol"), None), P()),
        check_vma=False,
    )
```

```python
import jax
import jax.numpy as jnp
from jax import lax
from jax.experimental import pallas as pl
from jax.experimental.pallas import tpu as pltpu
from jax.sharding import PartitionSpec as P

F32 = jnp.float32
BF16 = jnp.bfloat16
MESH = pl.DeviceIdType.MESH
W = 128
HALF = W // 2
NP = 8
RING = 4
PAIRS = 8
LAST = PAIRS - 1
COLS = 2 * W
EARLY = 2
LATE = 2
MIDDLE = 3


def split(value):
    high = value.astype(BF16)
    low = (value - high.astype(F32)).astype(BF16)
    return high, low


def product(left, right):
    contract = (((0,), (0,)), ((), ()))
    (left_high, left_low), (right_high, right_low) = split(left), split(right)
    total = lax.dot_general(left_high, right_high, contract, preferred_element_type=F32)
    total += lax.dot_general(left_low, right_high, contract, preferred_element_type=F32)
    total += lax.dot_general(left_high, right_low, contract, preferred_element_type=F32)
    return total


def aligned(start, size):
    return pl.ds(pl.multiple_of(start, size), size)


def kernel(
    a_hbm, lower_hbm, structure_ref, pivot_hbm, panel_hbm, diag_hbm,
    a_high, a_low, b_high, b_low, mask, ring_mask, gathered, partial,
    far, near, far_tile, near_tile, panel, correction, ring_lower, ring_panel,
    prow_in, x_in, y_in, pivot, diag,
    a_sem, lower_sem, pivot_sem, out_sem, gather_send, gather_recv,
    scatter_send, scatter_recv, reduce_send, reduce_recv, ring_sem,
):
    prow, pcol = lax.axis_index("prow"), lax.axis_index("pcol")
    z, core = prow // 2, prow % 2
    x, y = pcol // RING, pcol % RING

    def along_x(step):
        return (prow, ((x + step) % RING) * RING + y)

    def along_y(step):
        return (prow, x * RING + (y + step) % RING)

    def along_prow(step):
        return ((prow + step) % NP, pcol)

    def tile_of(step, which):
        return ((z + step) % RING) * 2 + which

    sibling = (tile_of(0, 1 - core), pcol)
    z_next = (tile_of(1, core), pcol)
    z_last = (tile_of(3, core), pcol)

    def send(source, target, send_sem, recv_sem, device):
        pltpu.make_async_remote_copy(
            src_ref=source, dst_ref=target, send_sem=send_sem, recv_sem=recv_sem,
            device_id=device, device_id_type=MESH,
        ).start()

    def await_bytes(ref, sem):
        pltpu.make_async_copy(ref, ref, sem).wait()

    barrier = pltpu.get_barrier_semaphore()
    partners = [along_prow(k) for k in range(1, NP)]
    partners += [along_x(k) for k in range(1, RING)]
    partners += [along_y(k) for k in range(1, RING)]
    for device in partners:
        pl.semaphore_signal(barrier, inc=1, device_id=device, device_id_type=MESH)

    for t in range(PAIRS):
        pltpu.make_async_copy(
            lower_hbm.at[:, pl.ds(t * COLS, COLS)], gathered.at[t, prow], lower_sem.at[min(t, 1)]
        ).start()
    for part in range(4):
        pltpu.make_async_copy(
            a_hbm.at[pl.ds(2 * part, 2)], partial.at[pl.ds(2 * part, 2)], a_sem.at[part]
        ).start()
    own_rows = aligned(prow * 32, 32)
    pltpu.make_async_copy(pivot_hbm.at[:, own_rows], pivot, pivot_sem).start()

    def member(tile):
        listed = jnp.where(structure_ref[...] == prow * 16 + tile, 1.0, 0.0).astype(F32)
        return jnp.broadcast_to(jnp.max(listed, axis=1, keepdims=True), mask.shape)

    mask[...] = member(pcol)
    for k in range(RING):
        ring_mask[0, k] = member(x * RING + k)
        ring_mask[1, k] = member(k * RING + y)

    await_bytes(gathered.at[0, prow], lower_sem.at[0])
    pl.semaphore_wait(barrier, len(partners))
    await_bytes(gathered.at[pl.ds(1, PAIRS - 1), prow], lower_sem.at[1])

    def gather_send_to(t, ref, which, recv, device):
        send(ref, ref, gather_send.at[which], recv, device)

    def gather_first(t):
        ref = gathered.at[t, prow]
        gather_send_to(t, ref, 0, gather_recv.at[t, 0], z_next)
        gather_send_to(t, ref, 1, gather_recv.at[t, 1], z_last)
        gather_send_to(t, ref, 2, gather_recv.at[t, 3], sibling)

    def gather_second(t):
        ref = gathered.at[t, tile_of(3, core)]
        await_bytes(ref, gather_recv.at[t, 0])
        gather_send_to(t, ref.at[pl.ds(0, HALF)], 5, gather_recv.at[t, 2], z_next)
        gather_send_to(t, ref, 3, gather_recv.at[t, 4], sibling)
        ref = gathered.at[t, tile_of(1, core)]
        await_bytes(ref, gather_recv.at[t, 1])
        gather_send_to(t, ref.at[pl.ds(HALF, HALF)], 6, gather_recv.at[t, 2], z_last)
        gather_send_to(t, ref, 4, gather_recv.at[t, 5], sibling)

    def gather_third(t):
        ref = gathered.at[t, tile_of(2, core)]
        await_bytes(ref, gather_recv.at[t, 2])
        gather_send_to(t, ref, 7, gather_recv.at[t, 6], sibling)

    def gather_wait(t):
        for k, step in enumerate((0, 3, 1, 2)):
            await_bytes(gathered.at[t, tile_of(step, 1 - core)], gather_recv.at[t, 3 + k])

    def multiply(t):
        for tile in range(NP):
            high, low = split(gathered[t, tile])
            b_high[tile * W:(tile + 1) * W] = high
            b_low[tile * W:(tile + 1) * W] = low

    def multiply_rows(h):
        def body(t):
            rows = pl.ds(h * 8 * W, 8 * W)
            total = jnp.dot(a_high[rows], b_high[...], preferred_element_type=F32)
            total += jnp.dot(a_low[rows], b_high[...], preferred_element_type=F32)
            total += jnp.dot(a_high[rows], b_low[...], preferred_element_type=F32)
            for n in range(8):
                i, j = h * 2 + n // 4, n % 4
                block = total[n * W:(n + 1) * W]
                partial[2 * t, i, j] = block[:, :W]
                partial[2 * t + 1, j, i] = block[:, W:]
        return body

    def multiply_first():
        @pl.loop(0, RING)
        def _(k):
            step = jnp.where(k == 0, 0, jnp.where(k == 1, 3, jnp.where(k == 2, 1, 2)))

            @pl.when(k == 3)
            def _():
                gather_second(1)
                gather_first(2)
                gather_third(0)

            chip = (z + step) % RING
            depth = aligned(chip * COLS, COLS)
            await_bytes(gathered.at[0, chip * 2 + 1 - core], gather_recv.at[0, 3 + k])
            for which in range(2):
                high, low = split(gathered[0, chip * 2 + which])
                b_high[which * W:(which + 1) * W] = high
                b_low[which * W:(which + 1) * W] = low

            high, low = b_high[0:COLS], b_low[0:COLS]

            @pl.loop(0, 2)
            def _(h):
                rows = aligned(h * 8 * W, 8 * W)
                total = jnp.dot(a_high[rows, depth], high, preferred_element_type=F32)
                total += jnp.dot(a_low[rows, depth], high, preferred_element_type=F32)
                total += jnp.dot(a_high[rows, depth], low, preferred_element_type=F32)
                for n in range(8):
                    i, j = h * 2 + n // 4, n % 4
                    block = total[n * W:(n + 1) * W]
                    partial[0, i, j] = block[:, :W] + jnp.where(k == 0, 0.0, partial[0, i, j])
                    partial[1, j, i] = block[:, W:] + jnp.where(k == 0, 0.0, partial[1, j, i])

    def routes(t):
        return (
            (2 * t, x, y, along_x, along_y),
            (2 * t + 1, y, x, along_y, along_x),
        )

    def scatter_send_to(t, which, source, target, device):
        send(source, target, scatter_send.at[which], scatter_recv.at[t, which // 2], device)

    def scatter_first(t):
        for b, u, v, first, second in routes(t):
            block = partial.at[b, (u + 2) % RING]
            scatter_send_to(t, 0, block.at[pl.ds(0, 2)], far.at[b, 0], first(1))
            scatter_send_to(t, 1, block.at[pl.ds(2, 2)], far.at[b, 1], first(3))

    def scatter_second(t):
        await_bytes(far.at[pl.ds(2 * t, 2)], scatter_recv.at[t, 0])
        for b, u, v, first, second in routes(t):
            up, down = (u + 1) % RING, (u + 3) % RING
            partial[b, up, 0:2] += far[b, 0]
            scatter_send_to(t, 2, partial.at[b, up], near.at[b, 0], first(1))
            partial[b, down, 2:4] += far[b, 1]
            scatter_send_to(t, 3, partial.at[b, down], near.at[b, 1], first(3))

    def scatter_third(t):
        await_bytes(near.at[pl.ds(2 * t, 2)], scatter_recv.at[t, 1])
        for b, u, v, first, second in routes(t):
            partial[b, u] += near[b, 0] + near[b, 1]

    def scatter_turn(t):
        for b, u, v, first, second in routes(t):
            block = partial.at[b, u, (v + 2) % RING]
            scatter_send_to(t, 4, block.at[pl.ds(0, HALF)], far_tile.at[b, 0], second(1))
            scatter_send_to(t, 5, block.at[pl.ds(HALF, HALF)], far_tile.at[b, 1], second(3))

    def scatter_fourth(t):
        await_bytes(far_tile.at[pl.ds(2 * t, 2)], scatter_recv.at[t, 2])
        for b, u, v, first, second in routes(t):
            up, down = (v + 1) % RING, (v + 3) % RING
            partial[b, u, up, 0:HALF] += far_tile[b, 0]
            scatter_send_to(t, 6, partial.at[b, u, up], near_tile.at[b, 0], second(1))
            partial[b, u, down, HALF:W] += far_tile[b, 1]
            scatter_send_to(t, 7, partial.at[b, u, down], near_tile.at[b, 1], second(3))

    def finish(t):
        await_bytes(near_tile.at[pl.ds(2 * t, 2)], scatter_recv.at[t, 3])
        for h, (b, u, v, first, second) in enumerate(routes(t)):
            total = partial[b, u, v] + near_tile[b, 0] + near_tile[b, 1]
            panel[t, :, h * W:(h + 1) * W] = -(total * mask[pl.ds(b, 1), :])
        columns = aligned(t * COLS, COLS)
        pltpu.make_async_copy(panel.at[t], panel_hbm.at[:, columns], out_sem.at[0]).start()

    def correct(t):
        for h in range(2):
            correction[t, h * W:(h + 1) * W] = lax.dot_general(
                gathered[t, prow, :, h * W:(h + 1) * W], panel[t, :, h * W:(h + 1) * W],
                (((0,), (0,)), ((), ())),
                precision=lax.Precision.HIGHEST, preferred_element_type=F32,
            )

    def ring_send():
        for t in range(EARLY, PAIRS):
            for h, (step, slot) in enumerate(((along_y, y), (along_x, x))):
                source = gathered.at[t, prow, :, pl.ds(h * W, W)]
                ring_lower[t - EARLY, h, slot] = source[...]
                for k in range(1, RING):
                    send(source, ring_lower.at[t - EARLY, h, slot], ring_sem.at[0], ring_sem.at[1], step(k))

    def correct_early(t):
        for h, (b, u, v, first, second) in enumerate(routes(t)):
            for k in range(RING):
                ring_panel[k] = -(partial[b, u, k] * ring_mask[h, k, pl.ds(b, 1), :])
            correction[t, h * W:(h + 1) * W] = product(
                ring_lower[t - EARLY, h].reshape(RING * W, W), ring_panel[...].reshape(RING * W, W)
            )

    def reduce_send_to(t, stage, source, target, device, sender=None):
        send(source, target, reduce_send.at[stage if sender is None else sender], reduce_recv.at[t, stage], device)

    def axes(t):
        even = t % 2 == 0
        x_devices, y_devices = [along_x(k)[1] for k in range(RING)], [along_y(k)[1] for k in range(RING)]
        u_devices = [(prow, jnp.where(even, a, b)) for a, b in zip(x_devices, y_devices)]
        v_devices = [(prow, jnp.where(even, b, a)) for a, b in zip(x_devices, y_devices)]
        return jnp.where(even, x, y), jnp.where(even, y, x), u_devices, v_devices

    def reduce_first(t):
        for k in range(1, NP):
            rows = aligned(((prow + k) % NP) * 32, 32)
            reduce_send_to(t, 0, correction.at[t, rows], prow_in.at[k, t], along_prow(k))

    def sum_prow(t):
        await_bytes(prow_in.at[pl.ds(1, NP - 1), t], reduce_recv.at[t, 0])
        total = correction[t, own_rows]
        for k in range(1, NP):
            total += prow_in[k, t]
        return total

    def spread_prow(t):
        for k in range(1, NP):
            ref = diag.at[t, own_rows]
            reduce_send_to(t, 4, ref, ref, along_prow(k))

    few = pl.ds(0, 8)

    def reduce_second(t):
        u, v, u_devices, v_devices = axes(t)
        x_in[0, t] = sum_prow(t)
        for k in range(1, RING):
            rows = aligned(((u + k) % RING) * 8, 8)
            reduce_send_to(t, 1, x_in.at[0, t, rows], x_in.at[k, t, few], u_devices[k])

    def reduce_third(t):
        u, v, u_devices, v_devices = axes(t)
        await_bytes(x_in.at[pl.ds(1, RING - 1), t, few], reduce_recv.at[t, 1])
        total = x_in[0, t, aligned(u * 8, 8)]
        for k in range(1, RING):
            total += x_in[k, t, few]
        y_in[v, t, few] = total
        for k in range(1, RING):
            ref = y_in.at[v, t, few]
            reduce_send_to(t, 2, ref, ref, v_devices[k])

    def reduce_fourth(t):
        u, v, u_devices, v_devices = axes(t)
        await_bytes(y_in.at[pl.ds(0, RING - 1), t, few], reduce_recv.at[t, 2])
        total = (y_in[0, t, few] + y_in[1, t, few]) + (y_in[2, t, few] + y_in[3, t, few])
        rows = aligned(prow * 32 + u * 8, 8)
        diag[t, rows] = pivot[t, aligned(u * 8, 8)] - total
        for k in range(1, RING):
            ref = diag.at[t, rows]
            reduce_send_to(t, 3, ref, ref, u_devices[k])

    def reduce_fifth(t):
        await_bytes(diag.at[t, pl.ds(0, 24)], reduce_recv.at[t, 3])
        spread_prow(t)

    def reduce_last(t):
        await_bytes(diag.at[t, pl.ds(0, 224)], reduce_recv.at[t, 4])
        pltpu.make_async_copy(diag.at[t], diag_hbm.at[t], out_sem.at[1]).start()

    def last_second():
        x_in[x, LAST] = sum_prow(LAST)
        for k in range(1, RING):
            ref = x_in.at[x, LAST]
            reduce_send_to(LAST, 1, ref, ref, along_x(k), 5)

    def last_third():
        await_bytes(x_in.at[pl.ds(0, RING - 1), LAST], reduce_recv.at[LAST, 1])
        y_in[y, LAST] = (x_in[0, LAST] + x_in[1, LAST]) + (x_in[2, LAST] + x_in[3, LAST])
        for k in range(1, RING):
            ref = y_in.at[y, LAST]
            reduce_send_to(LAST, 2, ref, ref, along_y(k), 6)

    def last_fourth():
        await_bytes(y_in.at[pl.ds(0, RING - 1), LAST], reduce_recv.at[LAST, 2])
        total = (y_in[0, LAST] + y_in[1, LAST]) + (y_in[2, LAST] + y_in[3, LAST])
        diag[LAST, own_rows] = pivot[LAST] - total
        spread_prow(LAST)

    def prepare():
        ring_send()

        @pl.loop(0, 128)
        def _(i):
            part = i // 32

            @pl.when(i % 32 == 0)
            def _():
                await_bytes(partial.at[pl.ds(2 * part, 2)], a_sem.at[part])

            rows = aligned(i * 16, 16)
            for r in range(NP):
                high, low = split(partial[i // 16, (i // 4) % 4, i % 4, pl.ds(r, 16, stride=8), :])
                a_high[rows, r * W:(r + 1) * W] = high
                a_low[rows, r * W:(r + 1) * W] = low

        await_bytes(pivot, pivot_sem)

    @pl.loop(-2, PAIRS + 7)
    def _(step):
        def at(lag, body, first=0, end=PAIRS):
            t = step - lag

            @pl.when((t >= first) & (t < end))
            def _():
                body(t)

        def once(when, body, *args):
            @pl.when(step == when)
            def _():
                body(*args)

        def late(when, body, first=LATE, end=PAIRS):
            @pl.when(step == when)
            def _():
                @pl.loop(first, end)
                def _(t):
                    body(t)

        at(0, gather_third, 1)
        at(10, reduce_last, 0, EARLY)
        at(9, reduce_fifth, 0, EARLY)
        at(8, reduce_fourth, 0, EARLY)
        at(7, reduce_third, 0, EARLY)
        at(6, reduce_second, 0, EARLY)
        late(LAST + 6, finish, LATE, MIDDLE)
        at(8, reduce_last, EARLY, LAST)
        at(7, reduce_fifth, EARLY, LAST)
        at(6, reduce_fourth, EARLY, LAST)
        at(5, reduce_third, EARLY, LAST)
        at(4, reduce_second, EARLY, LAST)
        once(LAST + 7, reduce_last, LAST)
        once(LAST + 6, last_fourth)
        once(LAST + 5, last_third)
        once(LAST + 4, last_second)
        late(LAST + 4, scatter_fourth, LATE, MIDDLE)
        late(LAST + 5, scatter_fourth, MIDDLE, PAIRS)
        late(LAST + 6, finish, MIDDLE, PAIRS)
        at(2, scatter_second)
        once(EARLY + 3, await_bytes, ring_lower.at[:, :, pl.ds(0, RING - 1)], ring_sem.at[1])
        late(LAST + 3, scatter_turn, LATE, LAST)
        at(3, scatter_third)
        at(3, scatter_turn, 0, LATE)
        at(3, scatter_turn, LAST)
        at(3, correct_early, EARLY)
        at(3, reduce_first, EARLY)
        at(4, scatter_fourth, 0, LATE)
        at(5, finish, 0, LATE)
        at(5, correct, 0, EARLY)
        at(5, reduce_first, 0, EARLY)
        once(0, multiply_first)
        at(0, gather_wait, 1)
        at(0, multiply, 1)
        at(0, multiply_rows(0), 1)
        at(-1, gather_second, 2)
        at(-2, gather_first, 3)
        at(0, multiply_rows(1), 1)
        at(0, scatter_first)
        at(-2, gather_first, 0, 2)
        once(-1, prepare)
        at(-1, gather_second, 0, 1)

    for which in range(8):
        ref = gathered.at[:, 0]
        await_bytes(ref.at[:, pl.ds(0, HALF)] if which in (5, 6) else ref, gather_send.at[which])
        buffer = (far, near, far_tile, near_tile)[which // 2]
        await_bytes(buffer.at[:, which % 2], scatter_send.at[which])
    await_bytes(ring_lower.at[:, :, pl.ds(0, RING - 1)], ring_sem.at[0])
    await_bytes(prow_in.at[pl.ds(1, NP - 1)], reduce_send.at[0])
    await_bytes(x_in.at[pl.ds(1, RING - 1), pl.ds(0, LAST), few], reduce_send.at[1])
    await_bytes(y_in.at[pl.ds(0, RING - 1), pl.ds(0, LAST), few], reduce_send.at[2])
    await_bytes(diag.at[pl.ds(0, LAST), pl.ds(0, 24)], reduce_send.at[3])
    await_bytes(diag.at[:, pl.ds(0, 224)], reduce_send.at[4])
    await_bytes(x_in.at[pl.ds(0, RING - 1), LAST], reduce_send.at[5])
    await_bytes(y_in.at[pl.ds(0, RING - 1), LAST], reduce_send.at[6])
    await_bytes(panel, out_sem.at[0])
    await_bytes(diag, out_sem.at[1])


def hand_over(panel_in, diag_in, panel_out, diag_out, panel_space, diag_space, sem):
    def parts(panel, diag):
        for k in range(4):
            yield panel.at[pl.ds(k * W // 4, W // 4)]
            yield diag.at[pl.ds(k * 2, 2)]

    stages = [list(parts(*refs)) for refs in (
        (panel_in, diag_in), (panel_space, diag_space), (panel_out, diag_out))]
    loads, stores = (
        [pltpu.make_async_copy(a, b, sem.at[n, k]) for k, (a, b) in enumerate(zip(*stages[n:n + 2]))]
        for n in range(2)
    )
    for load in loads:
        load.start()
    for load, store in zip(loads, stores):
        load.wait()
        store.start()
    for store in stores:
        store.wait()


def on_device(ancestor_inverse, lower_panel, structure, pivot_inverse):
    rows = ancestor_inverse.shape[0]
    blocks = ancestor_inverse.reshape(8, 4, 4, W, W)
    pivot_pairs = pivot_inverse.reshape(PAIRS, COLS, W)
    vmem = pl.BlockSpec(memory_space=pltpu.VMEM)
    hbm = pl.BlockSpec(memory_space=pl.ANY)
    depth = NP * W
    dma = pltpu.SemaphoreType.DMA
    out_shape = (
        jax.ShapeDtypeStruct(lower_panel.shape, F32),
        jax.ShapeDtypeStruct(pivot_pairs.shape, F32),
    )
    panel, diag = pl.pallas_call(
        kernel,
        out_shape=out_shape,
        in_specs=[hbm, hbm, vmem, hbm],
        out_specs=(hbm, hbm),
        scratch_shapes=[
            pltpu.VMEM((rows, depth), BF16),
            pltpu.VMEM((rows, depth), BF16),
            pltpu.VMEM((depth, COLS), BF16),
            pltpu.VMEM((depth, COLS), BF16),
            pltpu.VMEM((16, W), F32),
            pltpu.VMEM((2, RING, 16, W), F32),
            pltpu.VMEM((PAIRS, NP, W, COLS), F32),
            pltpu.VMEM((16, RING, RING, W, W), F32),
            pltpu.VMEM((16, 2, 2, W, W), F32),
            pltpu.VMEM((16, 2, 4, W, W), F32),
            pltpu.VMEM((16, 2, HALF, W), F32),
            pltpu.VMEM((16, 2, W, W), F32),
            pltpu.VMEM((PAIRS, W, COLS), F32),
            pltpu.VMEM((PAIRS, COLS, W), F32),
            pltpu.VMEM((PAIRS - EARLY, 2, RING, W, W), F32),
            pltpu.VMEM((RING, W, W), F32),
            pltpu.VMEM((NP, PAIRS, 32, W), F32),
            pltpu.VMEM((RING, PAIRS, 32, W), F32),
            pltpu.VMEM((RING, PAIRS, 32, W), F32),
            pltpu.VMEM((PAIRS, 32, W), F32),
            pltpu.VMEM((PAIRS, COLS, W), F32),
            dma((4,)),
            dma((2,)),
            dma,
            dma((2,)),
            dma((8,)),
            dma((PAIRS, 7)),
            dma((8,)),
            dma((PAIRS, 4)),
            dma((7,)),
            dma((PAIRS, 5)),
            dma((2,)),
        ],
        compiler_params=pltpu.CompilerParams(
            collective_id=0, has_side_effects=True, vmem_limit_bytes=62 * 1024 * 1024,
        ),
        cost_estimate=pl.CostEstimate(
            flops=2 * 3 * rows * depth * lower_panel.shape[1], bytes_accessed=12 << 20, transcendentals=0,
        ),
    )(blocks, lower_panel, structure, pivot_pairs)
    panel, diag = pl.pallas_call(
        hand_over,
        out_shape=out_shape,
        in_specs=[hbm, hbm],
        out_specs=(hbm, hbm),
        scratch_shapes=[
            pltpu.VMEM(out_shape[0].shape, F32), pltpu.VMEM(out_shape[1].shape, F32), dma((2, 8)),
        ],
        compiler_params=pltpu.CompilerParams(vmem_limit_bytes=62 * 1024 * 1024),
    )(panel, diag)
    return panel, diag.reshape(pivot_inverse.shape)


def solution(mesh):
    return jax.shard_map(
        on_device,
        mesh=mesh,
        in_specs=(P("prow", None, "pcol", None), P(("prow", "pcol"), None), P(), P()),
        out_specs=(P(("prow", "pcol"), None), P()),
        check_vma=False,
    )
```
